512 devices in a mesh: tile: 64 (over z, y), bands: 8 (over x, core).
Axes of the slice: x: 4, y: 4, z: 16, core: 2. Of those that a mesh axis runs over, the one named last changes fastest.
Arguments:
- scene_rows: bfloat16 [8, 8192, 768], P('bands', 'tile'), may hold values from -6 to 6
- row_dest: int32 [8192, 2], P('tile'), may hold values from 0 to 63, all different within a row; in each aligned block of 128 rows (0 to 127, 128 to 255, ...) at most 8 rows name the same one
- row_pos: int32 [8192, 2], P('tile'), may hold values from 0 to 1020
- along_taps: bfloat16 [8192, 2, 4], P('tile'), may hold values from 0.049804688 to 0.44921875
- across_taps: bfloat16 [8, 256, 8], P('bands'), may hold values from 0.019897461 to 0.29882812
- elevation: float32 [65536, 256], P(('tile', 'bands')), may hold values from -6 to 6
- pyramid_list: int32 [256, 3], P('tile'), may hold values from 0 to 63, as said below
Outputs:
- finished: bfloat16 [8, 65536, 256], P('bands', 'tile')
- pyramid: bfloat16 [8, 128, 256, 256], P('bands', 'tile')
The draws below stay inside these ranges and needn't reach their ends.
Inputs may be any that keep to these rules, and one draw needn't show every extreme that they name: `row_dest`: among the 128 rows of one scene owner the two owners of a row differ, and no tile owner is named more than 8 times; that many is reached. `pyramid_list`: column 0 is the owner of tile g's own strip or of the strip just before or after it; one owner hands at most 2 tiles to each neighbouring owner; some owner hands 2 tiles to its left neighbour and some owner (possibly another) hands 2 to its right; column 1 lies below 2, column 2 below 4.
All inputs are finite; a program needn't handle non-finite values.
Results may differ from the reference program's by a relative error of at most 0.0049.
The reference program's roundings to bfloat16 on the way (of `across_matrix` and `across`) count: a program that leaves them out, or rounds other values in their place, can miss the bound.
Values may be sent and summed in bfloat16 or wider, within the bound.
No kernel may reach another device: no remote copies, remote signals or barrier semaphores. Data moves between devices by JAX's collectives and lax.ppermute only.
A program may use at most 192 MiB of HBM per device.

```python
import math
import jax
import jax.numpy as jnp
import numpy as np
from jax import lax

TILE_WIDTH = 256
WSRC = 768
KA = 4
KX = 8
PYR_DEV = 2
ROWS_DEV = 128
TILES_DEV = 4
OWNERS = 64
BANDS = 8
CAP = 8
STRIP = 1024
ROWS_ALL = 8192
STRIP_ALL = 65536


def draw_pyramid_list(key, part):
    key = jax.random.fold_in(key, 11)
    keys = jax.random.split(key, 7)
    owner_ids = jnp.arange(OWNERS, dtype=jnp.int32)
    to_left = jax.random.randint(keys[0], (OWNERS,), 0, 3)
    to_right = jax.random.randint(keys[1], (OWNERS,), 0, 3)
    heavy_left = jax.random.randint(keys[2], (), 1, OWNERS - 1)
    heavy_right = jax.random.randint(keys[3], (), 1, OWNERS - 1)
    to_left = jnp.where(owner_ids == heavy_left, 2, to_left)
    to_right = jnp.where(owner_ids == heavy_right, 2, to_right)
    to_left = jnp.where(owner_ids == 0, 0, to_left)
    to_right = jnp.where(owner_ids == OWNERS - 1, 0, to_right)
    to_right = jnp.minimum(to_right, TILES_DEV - to_left)
    places = jnp.arange(TILES_DEV, dtype=jnp.int32)[None, :]
    offsets = jnp.where(places < to_left[:, None], -1, jnp.where(places < (to_left + to_right)[:, None], 1, 0))
    orders = jax.vmap(lambda each_key: jax.random.permutation(each_key, TILES_DEV))(jax.random.split(keys[4], OWNERS))
    offsets = jnp.take_along_axis(offsets, orders, axis=1)
    owners = owner_ids[:, None] + offsets
    level_slot = jax.random.randint(keys[5], (OWNERS, TILES_DEV), 0, PYR_DEV)
    quadrant = jax.random.randint(keys[6], (OWNERS, TILES_DEV), 0, 4)
    stacked = jnp.stack([owners, level_slot, quadrant], axis=2)
    return stacked.reshape(OWNERS * TILES_DEV, 3).astype(jnp.int32)


def touch_ends(entries, own_key, low, top_value):
    shape = entries.shape
    spot = [jax.random.randint(jax.random.fold_in(own_key, axis), (), 0, shape[axis]) for axis in range(len(shape))]
    entries = entries.at[tuple(spot)].set(low)
    longest = shape.index(max(shape))
    spot[longest] = (spot[longest] + 1) % shape[longest]
    return entries.at[tuple(spot)].set(top_value)


def block_levels(rng, extent, cuts, smallest, largest):
    factor_of, own = 1.0, jax.random.fold_in(rng, 6)
    for axis_at, shards_of in cuts:
        steps = jnp.exp(jax.random.uniform(jax.random.fold_in(own, axis_at), (shards_of,), jnp.float32, smallest / len(cuts), largest / len(cuts)))
        factor_of = factor_of * jnp.repeat(steps, extent[axis_at] // shards_of).reshape([-1 if axis == axis_at else 1 for axis in range(len(extent))])
    return factor_of


def shared_out(own_key, own, number, rows, amount, top, most, slope):
    sequence = jax.random.permutation(own_key, amount)
    crowded, ordinary = shares(amount, rows * top, most, slope, True), shares(amount, rows * top, most, slope, False)
    places = jnp.arange(amount)

    def named(tallies, turn):
        used = int((tallies > 0).sum())
        fixed = max(1, used // 4)
        shifted = fixed + (places - fixed + turn * (used - fixed)) % max(1, amount - fixed)
        return jnp.zeros((amount,), jnp.int32).at[sequence[jnp.where(places < fixed, places, shifted)]].set(jnp.asarray(tallies, jnp.int32))

    tallies = jnp.where(number % 4 == 0, named(crowded, number // 4), named(ordinary, number - number // 4 - 1))
    mixed = jax.random.permutation(jax.random.fold_in(own, 3), amount)
    donor, taker = mixed[0:amount // 2 * 2:2], mixed[1:amount // 2 * 2:2]
    margin = jnp.minimum(tallies[donor] - 1, most - tallies[taker]) // 2
    margin = jnp.where((donor == sequence[0]) | (taker == sequence[0]) | (tallies[taker] == 0), 0, jnp.maximum(margin, 0))
    shifted = jax.random.randint(jax.random.fold_in(own, 4), (amount // 2,), 0, 1 << 20) % (margin + 1)
    tallies = tallies.at[donor].add(-shifted).at[taker].add(shifted)
    items = jnp.searchsorted(jnp.cumsum(tallies), jnp.arange(rows * top), side="right").astype(jnp.int32)
    listing = items.reshape(top, rows).T
    listing = listing[jax.random.permutation(jax.random.fold_in(own, 1), rows)]
    turn = jax.random.randint(jax.random.fold_in(own, 2), (rows, 1), 0, top)
    return jnp.take_along_axis(listing, (jnp.arange(top)[None, :] + turn) % top, axis=1)


def shares(amount, total, bound, lean, full):
    loads = [(1 << 20) // math.isqrt(standing ** lean) + 1 for standing in range(1, amount + 1)]
    largest = bound if full else min(bound, max(-(-total // amount), total * loads[0] // sum(loads)))
    least = 1 if total - largest >= amount - 1 else 0
    counts, rest = [largest] + [least] * (amount - 1), total - largest - least * (amount - 1)
    while rest > 0:
        movable = [i for i in range(1, amount) if counts[i] < largest] or [i for i in range(1, amount) if counts[i] < bound]
        pool, remaining = sum([loads[i] for i in movable]), rest
        for i in movable:
            extra = min(bound - counts[i], max(1, remaining * loads[i] // pool), rest)
            counts[i] = counts[i] + extra
            rest = rest - extra
    return np.array(counts)


def gaussian(rng, dims, spread, limit, pieces=(), kind=jnp.bfloat16):
    loudness = block_levels(rng, dims, pieces, -0.22, 0.18) if pieces else 1.0
    entries = jax.random.normal(rng, dims, jnp.float32) * spread * loudness
    return jnp.minimum(jnp.maximum(entries, -limit), limit).astype(kind)


def setup_inputs(seed: int = 0) -> dict:
    key_list = jax.random.split(jax.random.key(seed), 8)
    scene_rows = gaussian(key_list[0], (BANDS, ROWS_ALL, WSRC), 1.0, 6.0, ((0, 8), (1, 64)))
    row_dest_keys = jax.random.split(jax.random.fold_in(key_list[1], 1), ROWS_ALL // ROWS_DEV)
    row_dest_turns = jax.random.permutation(jax.random.fold_in(key_list[1], 3), ROWS_ALL // ROWS_DEV)
    row_dest = jax.vmap(lambda own, number: shared_out(jax.random.fold_in(key_list[1], 2), own, number, ROWS_DEV, OWNERS, 2, CAP, 2))(row_dest_keys, row_dest_turns).reshape((ROWS_ALL, 2))
    row_pos = touch_ends(jax.random.randint(key_list[2], (ROWS_ALL, 2), 0, STRIP - KA + 1), jax.random.fold_in(key_list[2], 1), 0, STRIP - KA).astype(jnp.int32)
    along_taps = jnp.clip(0.049804688 + 0.39941406 * jax.random.uniform(key_list[3], (ROWS_ALL, 2, KA), jnp.float32) ** block_levels(key_list[3], (ROWS_ALL, 2, KA), ((0, 64),), -0.2, 0.2), 0.049804688, 0.44921875).astype(jnp.bfloat16)
    across_taps = jnp.clip(0.019897461 + 0.27893066 * jax.random.uniform(key_list[4], (BANDS, TILE_WIDTH, KX), jnp.float32) ** block_levels(key_list[4], (BANDS, TILE_WIDTH, KX), ((0, 8),), -0.2, 0.2), 0.019897461, 0.29882812).astype(jnp.bfloat16)
    elevation = gaussian(key_list[5], (STRIP_ALL, TILE_WIDTH), 1.0, 6.0, ((0, 512),), jnp.float32)
    pyramid_list = draw_pyramid_list(jax.random.fold_in(key_list[7], 71), 0)
    return {"scene_rows": scene_rows, "row_dest": row_dest, "row_pos": row_pos, "along_taps": along_taps, "across_taps": across_taps, "elevation": elevation, "pyramid_list": pyramid_list}


def across_build(taps):
    source = jnp.arange(WSRC, dtype=jnp.int32)[:, None, None]
    target = 3 * jnp.arange(TILE_WIDTH, dtype=jnp.int32)[None, :, None] - 2 + jnp.arange(KX, dtype=jnp.int32)[None, None, :]
    return lax.optimization_barrier(jnp.sum(jnp.where(source == target, taps.astype(jnp.float32)[None, :, :], jnp.float32(0.0)), axis=2))

def shade_of(padded):
    grid = jnp.pad(padded, ((0, 0), (1, 1)))
    grad_y = (grid[2:, 1:-1] - grid[:-2, 1:-1]) * 0.5
    grad_x = (grid[1:-1, 2:] - grid[1:-1, :-2]) * 0.5
    return (0.8660254 - 0.4 * grad_x - 0.3 * grad_y) / jnp.sqrt(1.0 + grad_x * grad_x + grad_y * grad_y)

def pyramid_downscale(output_tiles):
    half = output_tiles.shape[1] // 2
    values = output_tiles.astype(jnp.float32).reshape(output_tiles.shape[0], half, 2, half, 2)
    return lax.optimization_barrier(jnp.sum(values, axis=(2, 4))) * 0.25

def reference(scene_rows, row_dest, row_pos, along_taps, across_taps, elevation, pyramid_list):
    shade = shade_of(jnp.pad(elevation, ((1, 1), (0, 0))))
    dest = row_dest.reshape(-1).astype(jnp.int32)
    positions = row_pos.reshape(-1).astype(jnp.int32)
    taps = along_taps.reshape(-1, KA).astype(jnp.float32)
    output_tiles_full = STRIP_ALL // TILE_WIDTH
    codes = (pyramid_list[:, 0] * PYR_DEV * 4 + pyramid_list[:, 1] * 4 + pyramid_list[:, 2]).astype(jnp.int32)
    half = TILE_WIDTH // 2

    def one_band(index):
        rows = scene_rows[index]
        across_matrix = across_build(across_taps[index])
        across = jnp.dot(rows, across_matrix.astype(jnp.bfloat16), preferred_element_type=jnp.float32).astype(jnp.bfloat16)
        routed = jnp.repeat(across.astype(jnp.float32), 2, axis=0)
        resampled = jnp.zeros((STRIP_ALL, TILE_WIDTH), jnp.float32)
        for tap in range(KA):
            target = dest * STRIP + positions + tap
            resampled = resampled + jax.ops.segment_sum(taps[:, tap:tap + 1] * routed, target, num_segments=STRIP_ALL)
        finished = (resampled * shade).astype(jnp.bfloat16)
        halved_tiles = pyramid_downscale(finished.reshape(output_tiles_full, TILE_WIDTH, TILE_WIDTH))
        summed = jax.ops.segment_sum(halved_tiles, codes, num_segments=OWNERS * PYR_DEV * 4)
        summed = summed.reshape(OWNERS * PYR_DEV, 2, 2, half, half).transpose(0, 1, 3, 2, 4)
        return (finished, summed.reshape(OWNERS * PYR_DEV, TILE_WIDTH, TILE_WIDTH).astype(jnp.bfloat16))
    finished, pyramid = lax.map(one_band, jnp.arange(BANDS, dtype=jnp.int32))
    return (finished, pyramid)
```

```python
import jax
import jax.numpy as jnp
from jax import lax
from jax.experimental import pallas as pl
from jax.experimental.pallas import tpu as pltpu
from jax.sharding import PartitionSpec as P

TILE = 256
WSRC = 768
KA = 4
KX = 8
OWNERS = 64
CAP = 8
ROWS = 128
TILES = 4
HALF = 128
CHUNK = 2 * CAP + 2
GROUP = 8 * CHUNK
FIELDS = 2 + KA
PAYLOAD = 2 * HALF + 16
F32 = jnp.float32
BF16 = jnp.bfloat16
I32 = jnp.int32
VMEM = pl.BlockSpec(memory_space=pltpu.VMEM)
SMEM = pl.BlockSpec(memory_space=pltpu.SMEM)
PARAMS = pltpu.CompilerParams(vmem_limit_bytes=24 * 1024 * 1024)


def iota(shape, axis):
    return lax.broadcasted_iota(I32, shape, axis)


def dot(a, b):
    return jnp.dot(a, b, preferred_element_type=F32)


def dot_t(a, b):
    return lax.dot_general(a, b, (((1,), (1,)), ((), ())), preferred_element_type=F32)


def ones_where(mask):
    return jnp.where(mask, F32(1), F32(0))


def prep_kernel(rows_ref, dest_ref, pos_ref, along_ref, across_ref, out_ref):
    taps = across_ref[...].astype(F32)
    products = []
    for half in range(2):
        first, live = (0, 0) if half == 0 else (256, 368)
        shape = (400, HALF)
        offset = iota(shape, 0) + live - 3 * (iota(shape, 1) + half * HALF) + 2
        matrix = jnp.zeros(shape, F32)
        for tap in range(KX):
            matrix = jnp.where(offset == tap, taps[tap : tap + 1, half * HALF : (half + 1) * HALF], matrix)
        matrix = matrix.astype(BF16)
        empty = jnp.zeros((112, HALF), BF16)
        matrix = jnp.concatenate([matrix, empty] if half == 0 else [empty, matrix], axis=0)
        products.append(dot(rows_ref[:, first : first + 512], matrix).astype(BF16))
    products = jnp.concatenate(products, axis=0)

    owner = iota((OWNERS, ROWS), 0)
    d0, d1 = dest_ref[0:1, :], dest_ref[1:2, :]
    on0, on1 = ones_where(owner == d0), ones_where(owner == d1)
    b0, b1 = on0.astype(BF16), on1.astype(BF16)
    earlier = ones_where(iota((ROWS, ROWS), 0) < iota((ROWS, ROWS), 1)).astype(BF16)
    rank0 = jnp.sum(on0 * dot(b0, earlier), axis=0, keepdims=True).astype(I32)
    before1 = dot(b1, earlier) + dot(b0, jnp.ones((ROWS, ROWS), BF16))
    rank1 = jnp.sum(on1 * before1, axis=0, keepdims=True).astype(I32)

    slot = iota((CAP, ROWS), 0)
    meta = jnp.zeros((OWNERS, HALF), F32)
    for t, (on, rank) in enumerate(((b0, rank0), (b1, rank1))):
        position = pos_ref[t : t + 1, :]
        along = along_ref[t].astype(F32)
        fields = [(position >> 4).astype(F32), (position & 15).astype(F32)]
        fields += [along[k : k + 1, :] for k in range(KA)]
        spread = [jnp.where(slot == rank, field, F32(0)) for field in fields]
        spread.append(jnp.zeros((HALF - FIELDS * CAP, ROWS), F32))
        meta = meta + dot_t(on, jnp.concatenate(spread, axis=0).astype(BF16))
    meta = meta.astype(BF16)

    base0, base1 = d0 * CHUNK + 2 * rank0, d1 * CHUNK + 2 * rank1
    row = iota((GROUP, ROWS), 0)
    row_o, col_o = iota((GROUP, OWNERS), 0), iota((GROUP, OWNERS), 1)
    for g in range(OWNERS // 8):
        n0, n1 = base0 - g * GROUP, base1 - g * GROUP
        left = ones_where((row == n0) | (row == n1))
        right = ones_where((row == n0 + 1) | (row == n1 + 1))
        pick = jnp.concatenate([left, right], axis=1).astype(BF16)
        place = ones_where(row_o + g * GROUP == col_o * CHUNK + 2 * CAP).astype(BF16)
        out_ref[g * GROUP : (g + 1) * GROUP, :] = (dot(pick, products) + dot(place, meta)).astype(BF16)


def shade_kernel(z_ref, before_ref, after_ref, out_ref):
    z = z_ref[...]
    shape = z.shape
    row, col = iota(shape, 0), iota(shape, 1)
    up = jnp.where(row == 0, before_ref[...], pltpu.roll(z, 1, 0))
    down = jnp.where(row == shape[0] - 1, after_ref[...], pltpu.roll(z, shape[0] - 1, 0))
    left = jnp.where(col == 0, F32(0), pltpu.roll(z, 1, 1))
    right = jnp.where(col == shape[1] - 1, F32(0), pltpu.roll(z, shape[1] - 1, 1))
    grad_y = (down - up) * 0.5
    grad_x = (right - left) * 0.5
    shade = (0.8660254 - 0.4 * grad_x - 0.3 * grad_y) / jnp.sqrt(1.0 + grad_x * grad_x + grad_y * grad_y)
    out_ref[...] = shade.astype(BF16)


def main_kernel(recv_ref, mine_ref, theirs_ref, list_ref, out_ref, part_ref, up_ref, down_ref, across_ref, meta_ref):
    row, col = iota((GROUP, GROUP), 0), iota((GROUP, GROUP), 1)
    slot = row & 63
    target = jnp.where(
        row < 2 * 64,
        CHUNK * (slot >> 3) + 2 * (slot & 7) + (row >> 6),
        jnp.where(row < 2 * 64 + 8, CHUNK * slot + 2 * CAP, -1),
    )
    pick = ones_where(col == target).astype(BF16)
    for g in range(OWNERS // 8):
        parts = dot(pick, recv_ref[g * GROUP : (g + 1) * GROUP, :])
        across_ref[g * 64 : (g + 1) * 64, :HALF] = parts[:64].astype(BF16)
        across_ref[g * 64 : (g + 1) * 64, HALF:] = parts[64:128].astype(BF16)
        meta_ref[g * 8 : (g + 1) * 8, :] = parts[128:136]
    slots = OWNERS * CAP
    meta = meta_ref[...]
    rolled = [meta] + [pltpu.roll(meta, HALF - CAP * f, 1) for f in range(1, FIELDS)]
    spread = ones_where(iota((HALF, slots), 0) == (iota((HALF, slots), 1) & 7)).astype(BF16)
    wide = dot(jnp.concatenate(rolled, axis=0).astype(BF16), spread)
    own_lane = iota((OWNERS, slots), 0) == (iota((OWNERS, slots), 1) >> 3)
    fields = [
        jnp.sum(jnp.where(own_lane, wide[f * OWNERS : (f + 1) * OWNERS], F32(0)), axis=0, keepdims=True)
        for f in range(FIELDS)
    ]
    block, inner = fields[0].astype(I32), fields[1].astype(I32)
    diff = iota((16, slots), 0) - inner
    here, after = jnp.zeros((16, slots), F32), jnp.zeros((16, slots), F32)
    for tap in range(KA):
        here = jnp.where(diff == tap, fields[2 + tap], here)
        after = jnp.where(diff + 16 == tap, fields[2 + tap], after)
    block = jnp.broadcast_to(block, (16, slots))

    tile_me = lax.axis_index("tile")
    band_me = lax.axis_index("bands")
    core_me, x_me = lax.rem(band_me, 2), lax.div(band_me, 2)
    rows_of = ones_where(iota((HALF, TILE), 0) == (iota((HALF, TILE), 1) >> 1)).astype(BF16)
    cols_of = ones_where((iota((TILE, HALF), 0) >> 1) == iota((TILE, HALF), 1)).astype(BF16)
    part_ref[...] = jnp.zeros(part_ref.shape, F32)
    up_ref[...] = jnp.zeros(up_ref.shape, BF16)
    down_ref[...] = jnp.zeros(down_ref.shape, BF16)
    across = across_ref[...]
    counts = [jnp.int32(0), jnp.int32(0)]
    codes = [[jnp.int32(0), jnp.int32(0)], [jnp.int32(0), jnp.int32(0)]]
    for tile in range(TILES):
        weights = jnp.concatenate(
            [
                jnp.where(block == p, here, jnp.where(block == p - 1, after, F32(0))).astype(BF16)
                for p in range(16 * tile, 16 * tile + 16)
            ],
            axis=0,
        )
        resampled = dot(weights, across)
        mine = mine_ref[tile ^ x_me].astype(F32)
        theirs = theirs_ref[tile ^ x_me].astype(F32)
        top = jnp.where(core_me == 0, mine, theirs)
        bottom = jnp.where(core_me == 0, theirs, mine)
        finished = (resampled * jnp.concatenate([top, bottom], axis=0)).astype(BF16)
        out_ref[tile * TILE : (tile + 1) * TILE, :] = finished
        pairs = dot(rows_of, finished)
        high = pairs.astype(BF16)
        low = (pairs - high.astype(F32)).astype(BF16)
        reduced = (dot(high, cols_of) + dot(low, cols_of)) * 0.25
        offset = list_ref[tile, 0] - tile_me
        code = list_ref[tile, 1] * 4 + list_ref[tile, 2]

        @pl.when(offset == 0)
        def _(reduced=reduced, code=code):
            part_ref[code] = part_ref[code] + reduced

        for way, (step, ref) in enumerate(((1, up_ref), (-1, down_ref))):
            goes = offset == step
            rank = jnp.minimum(counts[way], 1)

            @pl.when(goes)
            def _(reduced=reduced, rank=rank, ref=ref):
                ref[pl.ds(pl.multiple_of(rank * HALF, HALF), HALF), :] = reduced.astype(BF16)

            for s in range(2):
                codes[way][s] = jnp.where(goes & (rank == s), code + 1, codes[way][s])
            counts[way] = counts[way] + goes.astype(I32)
    eighth = iota((16, HALF), 0) < 8
    for way, ref in enumerate((up_ref, down_ref)):
        ref[2 * HALF :, :] = jnp.where(eighth, codes[way][0], codes[way][1]).astype(F32).astype(BF16)


def combine_kernel(part_ref, up_ref, down_ref, out_ref):
    arrived = []
    for ref in (up_ref, down_ref):
        codes = ref[2 * HALF :, :].astype(F32)
        for s in range(2):
            arrived.append((codes[8 * s : 8 * s + 1], ref[s * HALF : (s + 1) * HALF, :].astype(F32)))
    for place in range(8):
        total = part_ref[place]
        for code, tile in arrived:
            total = total + jnp.where(code == F32(place + 1), tile, F32(0))
        level, quadrant = divmod(place, 4)
        top, left = quadrant // 2 * HALF, quadrant % 2 * HALF
        out_ref[level, top : top + HALF, left : left + HALF] = total.astype(BF16)


def call(kernel, outs, ins, scratch=(), cost=None):
    return pl.pallas_call(
        kernel,
        out_shape=outs,
        in_specs=ins,
        out_specs=jax.tree.map(lambda _: VMEM, outs),
        scratch_shapes=scratch,
        compiler_params=PARAMS,
        cost_estimate=cost,
    )


def shift(value, axes, by):
    size = lax.axis_size(axes)
    return lax.ppermute(value, axes, [(i, i + by) for i in range(size) if 0 <= i + by < size])


def exchange(value, mask):
    return lax.ppermute(value, "bands", [(i, i ^ mask) for i in range(lax.axis_size("bands"))])


def shards(scene_rows, row_dest, row_pos, along_taps, across_taps, elevation, pyramid_list):
    shape = jax.ShapeDtypeStruct
    outgoing = call(prep_kernel, shape((OWNERS * CHUNK, HALF), BF16), [VMEM] * 5)(
        scene_rows[0],
        row_dest.T,
        row_pos.T,
        along_taps.transpose(1, 2, 0),
        across_taps[0].T,
    )
    outgoing, elevation = lax.optimization_barrier((outgoing, elevation))
    units = outgoing.reshape(OWNERS * CHUNK // 2, 2, HALF)
    received = lax.all_to_all(units, "tile", split_axis=0, concat_axis=0, tiled=True)
    received = received.reshape(OWNERS * CHUNK, HALF)

    both = ("tile", "bands")
    before = shift(elevation[ROWS - 1 :], both, 1)
    after = shift(elevation[:1], both, -1)
    shade = call(shade_kernel, shape((ROWS, TILE), BF16), [VMEM] * 3)(elevation, before, after)
    mine = jnp.stack([shade, exchange(shade, 2), exchange(shade, 4), exchange(shade, 6)])
    theirs = exchange(mine, 1)

    finished, part, up, down = call(
        main_kernel,
        (
            shape((TILES * TILE, TILE), BF16),
            shape((8, HALF, HALF), F32),
            shape((PAYLOAD, HALF), BF16),
            shape((PAYLOAD, HALF), BF16),
        ),
        [VMEM, VMEM, VMEM, SMEM],
        [pltpu.VMEM((OWNERS * CAP, TILE), BF16), pltpu.VMEM((OWNERS, HALF), F32)],
    )(received, mine, theirs, pyramid_list)
    pyramid = call(combine_kernel, shape((2, TILE, TILE), BF16), [VMEM] * 3)(
        part, shift(up, "tile", 1), shift(down, "tile", -1)
    )
    return (finished[None], pyramid[None])


def solution(mesh):
    in_specs = (
        P("bands", "tile", None),
        P("tile", None),
        P("tile", None),
        P("tile", None, None),
        P("bands", None, None),
        P(("tile", "bands"), None),
        P("tile", None),
    )
    out_specs = (P("bands", "tile", None), P("bands", "tile", None, None))
    return jax.shard_map(shards, mesh=mesh, in_specs=in_specs, out_specs=out_specs, check_vma=False)
```

```python
import jax
import jax.numpy as jnp
from jax import lax
from jax.experimental import pallas as pl
from jax.experimental.pallas import tpu as pltpu
from jax.sharding import PartitionSpec as P

TILE = 256
WSRC = 768
KA = 4
KX = 8
OWNERS = 64
CAP = 8
ROWS = 128
TILES = 4
HALF = 128
CHUNK = 2 * CAP + 2
GROUP = 8 * CHUNK
FIELDS = 2 + KA
PAYLOAD = 2 * HALF + 16
F32 = jnp.float32
BF16 = jnp.bfloat16
I32 = jnp.int32
VMEM = pl.BlockSpec(memory_space=pltpu.VMEM)
SMEM = pl.BlockSpec(memory_space=pltpu.SMEM)
PARAMS = pltpu.CompilerParams(vmem_limit_bytes=24 * 1024 * 1024)


def iota(shape, axis):
    return lax.broadcasted_iota(I32, shape, axis)


def dot(a, b):
    return jnp.dot(a, b, preferred_element_type=F32)


def dot_t(a, b):
    return lax.dot_general(a, b, (((1,), (1,)), ((), ())), preferred_element_type=F32)


def ones_where(mask):
    return jnp.where(mask, F32(1), F32(0))


def prep_kernel(rows_ref, dest_ref, pos_ref, along_ref, across_ref, out_ref):
    taps = across_ref[...].astype(F32)
    products = []
    for half in range(2):
        first, live = (0, 0) if half == 0 else (256, 368)
        shape = (400, HALF)
        offset = iota(shape, 0) + live - 3 * (iota(shape, 1) + half * HALF) + 2
        matrix = jnp.zeros(shape, F32)
        for tap in range(KX):
            matrix = jnp.where(offset == tap, taps[tap : tap + 1, half * HALF : (half + 1) * HALF], matrix)
        matrix = matrix.astype(BF16)
        empty = jnp.zeros((112, HALF), BF16)
        matrix = jnp.concatenate([matrix, empty] if half == 0 else [empty, matrix], axis=0)
        products.append(dot(rows_ref[:, first : first + 512], matrix).astype(BF16))
    products = jnp.concatenate(products, axis=0)

    owner = iota((OWNERS, ROWS), 0)
    d0, d1 = dest_ref[0:1, :], dest_ref[1:2, :]
    on0, on1 = ones_where(owner == d0), ones_where(owner == d1)
    b0, b1 = on0.astype(BF16), on1.astype(BF16)
    earlier = ones_where(iota((ROWS, ROWS), 0) < iota((ROWS, ROWS), 1)).astype(BF16)
    rank0 = jnp.sum(on0 * dot(b0, earlier), axis=0, keepdims=True).astype(I32)
    before1 = dot(b1, earlier) + dot(b0, jnp.ones((ROWS, ROWS), BF16))
    rank1 = jnp.sum(on1 * before1, axis=0, keepdims=True).astype(I32)

    slot = iota((CAP, ROWS), 0)
    meta = jnp.zeros((OWNERS, HALF), F32)
    for t, (on, rank) in enumerate(((b0, rank0), (b1, rank1))):
        position = pos_ref[t : t + 1, :]
        along = along_ref[t].astype(F32)
        fields = [(position >> 4).astype(F32), (position & 15).astype(F32)]
        fields += [along[k : k + 1, :] for k in range(KA)]
        spread = [jnp.where(slot == rank, field, F32(0)) for field in fields]
        spread.append(jnp.zeros((HALF - FIELDS * CAP, ROWS), F32))
        meta = meta + dot_t(on, jnp.concatenate(spread, axis=0).astype(BF16))
    meta = meta.astype(BF16)

    base0, base1 = d0 * CHUNK + 2 * rank0, d1 * CHUNK + 2 * rank1
    row = iota((GROUP, ROWS), 0)
    row_o, col_o = iota((GROUP, OWNERS), 0), iota((GROUP, OWNERS), 1)
    for g in range(OWNERS // 8):
        n0, n1 = base0 - g * GROUP, base1 - g * GROUP
        left = ones_where((row == n0) | (row == n1))
        right = ones_where((row == n0 + 1) | (row == n1 + 1))
        pick = jnp.concatenate([left, right], axis=1).astype(BF16)
        place = ones_where(row_o + g * GROUP == col_o * CHUNK + 2 * CAP).astype(BF16)
        out_ref[g * GROUP : (g + 1) * GROUP, :] = (dot(pick, products) + dot(place, meta)).astype(BF16)


def shade_of(z, up, down):
    col = iota(z.shape, 1)
    left = jnp.where(col == 0, F32(0), pltpu.roll(z, 1, 1))
    right = jnp.where(col == z.shape[1] - 1, F32(0), pltpu.roll(z, z.shape[1] - 1, 1))
    grad_y = (down - up) * 0.5
    grad_x = (right - left) * 0.5
    return (0.8660254 - 0.4 * grad_x - 0.3 * grad_y) / jnp.sqrt(1.0 + grad_x * grad_x + grad_y * grad_y)


def shade_kernel(z_ref, beside_ref, out_ref):
    z = z_ref[...]
    out_ref[:ROWS, :] = shade_of(z, pltpu.roll(z, 1, 0), pltpu.roll(z, ROWS - 1, 0)).astype(BF16)
    row = iota((8, TILE), 0)
    border = jnp.where(row < 2, z[:8], jnp.where(row < 4, pltpu.roll(z[ROWS - 8 :], 4, 0), F32(0)))
    edge = jnp.where(lax.axis_index("bands") == 0, beside_ref[:1], beside_ref[ROWS - 1 :])
    border = jnp.where(row == 4, edge, border)
    high = border.astype(BF16).astype(F32)
    out_ref[ROWS:, :] = jnp.concatenate([high, border - high], axis=0).astype(BF16)


def resample_kernel(recv_ref, out_ref, across_ref, meta_ref):
    row, col = iota((GROUP, GROUP), 0), iota((GROUP, GROUP), 1)
    slot = row & 63
    target = jnp.where(
        row < 2 * 64,
        CHUNK * (slot >> 3) + 2 * (slot & 7) + (row >> 6),
        jnp.where(row < 2 * 64 + 8, CHUNK * slot + 2 * CAP, -1),
    )
    pick = ones_where(col == target).astype(BF16)
    for g in range(OWNERS // 8):
        parts = dot(pick, recv_ref[g * GROUP : (g + 1) * GROUP, :])
        across_ref[g * 64 : (g + 1) * 64, :HALF] = parts[:64].astype(BF16)
        across_ref[g * 64 : (g + 1) * 64, HALF:] = parts[64:128].astype(BF16)
        meta_ref[g * 8 : (g + 1) * 8, :] = parts[128:136]
    slots = OWNERS * CAP
    meta = meta_ref[...]
    rolled = [meta] + [pltpu.roll(meta, HALF - CAP * f, 1) for f in range(1, FIELDS)]
    spread = ones_where(iota((HALF, slots), 0) == (iota((HALF, slots), 1) & 7)).astype(BF16)
    wide = dot(jnp.concatenate(rolled, axis=0).astype(BF16), spread)
    own_lane = iota((OWNERS, slots), 0) == (iota((OWNERS, slots), 1) >> 3)
    fields = [
        jnp.sum(jnp.where(own_lane, wide[f * OWNERS : (f + 1) * OWNERS], F32(0)), axis=0, keepdims=True)
        for f in range(FIELDS)
    ]
    block, inner = fields[0].astype(I32), fields[1].astype(I32)
    diff = iota((16, slots), 0) - inner
    here, after = jnp.zeros((16, slots), F32), jnp.zeros((16, slots), F32)
    for tap in range(KA):
        here = jnp.where(diff == tap, fields[2 + tap], here)
        after = jnp.where(diff + 16 == tap, fields[2 + tap], after)
    block = jnp.broadcast_to(block, (16, slots))
    across = across_ref[...]
    for tile in range(TILES):
        weights = jnp.concatenate(
            [
                jnp.where(block == p, here, jnp.where(block == p - 1, after, F32(0))).astype(BF16)
                for p in range(16 * tile, 16 * tile + 16)
            ],
            axis=0,
        )
        out_ref[tile * TILE : (tile + 1) * TILE, :] = dot(weights, across)


def finish_kernel(
    resampled_ref,
    mine_ref,
    theirs_ref,
    list_ref,
    out_ref,
    part_ref,
    up_ref,
    down_ref,
    border_ref,
    reduced_ref,
    column_ref,
    stage_ref,
    sems,
):
    tile_me = lax.axis_index("tile")
    band_me = lax.axis_index("bands")
    core_me, x_me = lax.rem(band_me, 2), lax.div(band_me, 2)

    def two_blocks(tile, rows):
        mine = mine_ref[tile ^ x_me, rows, :].astype(F32)
        theirs = theirs_ref[tile ^ x_me, rows, :].astype(F32)
        return jnp.where(core_me == 0, mine, theirs), jnp.where(core_me == 0, theirs, mine)

    for tile in range(TILES):
        for i, part in enumerate(two_blocks(tile, slice(ROWS, ROWS + 16))):
            exact = part[:8] + part[8:]
            for f in range(5):
                border_ref[f, 2 * tile + i : 2 * tile + i + 1, :] = exact[f : f + 1]
    first, second, before_last, last, edge = [border_ref[f] for f in range(5)]
    row = iota((8, TILE), 0)
    first_shade = shade_of(first, jnp.where(row == 0, edge[7:8], pltpu.roll(last, 1, 0)), second)
    last_shade = shade_of(last, before_last, jnp.where(row == 7, edge[0:1], pltpu.roll(first, 7, 0)))

    cols_of = ones_where((iota((TILE, HALF), 0) >> 1) == iota((TILE, HALF), 1)).astype(BF16)
    copies = []
    for tile in range(TILES):
        shade = []
        for i, block in enumerate(two_blocks(tile, slice(0, ROWS))):
            b = 2 * tile + i
            shade.append(jnp.where(row == 0, first_shade[b : b + 1], block[:8]))
            shade.append(block[8:-8])
            shade.append(jnp.where(row == 7, last_shade[b : b + 1], block[-8:]))
        rows = slice(tile * TILE, (tile + 1) * TILE)
        finished = (resampled_ref[rows, :] * jnp.concatenate(shade, axis=0)).astype(BF16)
        stage_ref[rows, :] = finished
        copy = pltpu.make_async_copy(stage_ref.at[rows], out_ref.at[rows], sems.at[tile])
        copy.start()
        copies.append(copy)
        column_ref[...] = dot(finished, cols_of)
        reduced_ref[tile] = (column_ref[pl.ds(0, HALF, stride=2), :] + column_ref[pl.ds(1, HALF, stride=2), :]) * 0.25

    part_ref[...] = jnp.zeros(part_ref.shape, F32)
    up_ref[...] = jnp.zeros(up_ref.shape, BF16)
    down_ref[...] = jnp.zeros(down_ref.shape, BF16)
    counts = [jnp.int32(0), jnp.int32(0)]
    codes = [[jnp.int32(0), jnp.int32(0)], [jnp.int32(0), jnp.int32(0)]]
    for tile in range(TILES):
        offset = list_ref[tile, 0] - tile_me
        code = list_ref[tile, 1] * 4 + list_ref[tile, 2]

        @pl.when(offset == 0)
        def _(tile=tile, code=code):
            part_ref[code] = part_ref[code] + reduced_ref[tile]

        for way, (step, ref) in enumerate(((1, up_ref), (-1, down_ref))):
            goes = offset == step
            rank = jnp.minimum(counts[way], 1)

            @pl.when(goes)
            def _(tile=tile, rank=rank, ref=ref):
                ref[pl.ds(pl.multiple_of(rank * HALF, HALF), HALF), :] = reduced_ref[tile].astype(BF16)

            for s in range(2):
                codes[way][s] = jnp.where(goes & (rank == s), code + 1, codes[way][s])
            counts[way] = counts[way] + goes.astype(I32)
    eighth = iota((16, HALF), 0) < 8
    for way, ref in enumerate((up_ref, down_ref)):
        ref[2 * HALF :, :] = jnp.where(eighth, codes[way][0], codes[way][1]).astype(F32).astype(BF16)
    for copy in copies:
        copy.wait()


def combine_kernel(part_ref, up_ref, down_ref, out_ref):
    arrived = []
    for ref in (up_ref, down_ref):
        codes = ref[2 * HALF :, :].astype(F32)
        for s in range(2):
            arrived.append((codes[8 * s : 8 * s + 1], ref[s * HALF : (s + 1) * HALF, :].astype(F32)))
    for place in range(8):
        total = part_ref[place]
        for code, tile in arrived:
            total = total + jnp.where(code == F32(place + 1), tile, F32(0))
        level, quadrant = divmod(place, 4)
        top, left = quadrant // 2 * HALF, quadrant % 2 * HALF
        out_ref[level, top : top + HALF, left : left + HALF] = total.astype(BF16)


def call(kernel, outs, ins, scratch=(), cost=None, params=PARAMS, out_specs=None):
    return pl.pallas_call(
        kernel,
        out_shape=outs,
        in_specs=ins,
        out_specs=out_specs or jax.tree.map(lambda _: VMEM, outs),
        scratch_shapes=scratch,
        compiler_params=params,
        cost_estimate=cost,
    )


def shift(value, axes, by):
    size = lax.axis_size(axes)
    return lax.ppermute(value, axes, [(i, i + by) for i in range(size) if 0 <= i + by < size])


def exchange(value, mask):
    return lax.ppermute(value, "bands", [(i, i ^ mask) for i in range(lax.axis_size("bands"))])


def shards(scene_rows, row_dest, row_pos, along_taps, across_taps, elevation, pyramid_list):
    shape = jax.ShapeDtypeStruct
    outgoing = call(prep_kernel, shape((OWNERS * CHUNK, HALF), BF16), [VMEM] * 5, params=pltpu.CompilerParams(vmem_limit_bytes=60 * 1024 * 1024))(
        scene_rows[0],
        row_dest.T,
        row_pos.T,
        along_taps.transpose(1, 2, 0),
        across_taps[0].T,
    )
    both, last = ("tile", "bands"), lax.axis_size("bands") - 1
    owners = [last * t + t for t in range(lax.axis_size("tile"))]
    pairs = list(zip(owners[1:], owners[:-1])) + [(i + last, j + last) for i, j in zip(owners[:-1], owners[1:])]
    beside = lax.ppermute(elevation, both, pairs)
    outgoing, beside = lax.optimization_barrier((outgoing, beside))
    units = outgoing.reshape(OWNERS * CHUNK // 2, 2, HALF)
    received = lax.all_to_all(units, "tile", split_axis=0, concat_axis=0, tiled=True)
    received = received.reshape(OWNERS * CHUNK, HALF)

    shade = call(shade_kernel, shape((ROWS + 16, TILE), BF16), [VMEM] * 2)(elevation, beside)
    mine = jnp.stack([shade, exchange(shade, 2), exchange(shade, 4), exchange(shade, 6)])
    theirs = exchange(mine, 1)
    resampled = call(
        resample_kernel,
        shape((TILES * TILE, TILE), F32),
        [VMEM],
        [pltpu.VMEM((OWNERS * CAP, TILE), BF16), pltpu.VMEM((OWNERS, HALF), F32)],
        pl.CostEstimate(flops=400_000_000, bytes_accessed=1_500_000, transcendentals=0),
    )(received)
    finished, part, up, down = call(
        finish_kernel,
        (
            shape((TILES * TILE, TILE), BF16),
            shape((8, HALF, HALF), F32),
            shape((PAYLOAD, HALF), BF16),
            shape((PAYLOAD, HALF), BF16),
        ),
        [VMEM, VMEM, VMEM, SMEM],
        [
            pltpu.VMEM((5, 8, TILE), F32),
            pltpu.VMEM((TILES, HALF, HALF), F32),
            pltpu.VMEM((TILE, HALF), F32),
            pltpu.VMEM((TILES * TILE, TILE), BF16),
            pltpu.SemaphoreType.DMA((TILES,)),
        ],
        out_specs=(pl.BlockSpec(memory_space=pl.ANY), VMEM, VMEM, VMEM),
    )(resampled, mine, theirs, pyramid_list)
    pyramid = call(combine_kernel, shape((2, TILE, TILE), BF16), [VMEM] * 3)(
        part, shift(up, "tile", 1), shift(down, "tile", -1)
    )
    return (finished[None], pyramid[None])


def solution(mesh):
    in_specs = (
        P("bands", "tile", None),
        P("tile", None),
        P("tile", None),
        P("tile", None, None),
        P("bands", None, None),
        P(("tile", "bands"), None),
        P("tile", None),
    )
    out_specs = (P("bands", "tile", None), P("bands", "tile", None, None))
    return jax.shard_map(shards, mesh=mesh, in_specs=in_specs, out_specs=out_specs, check_vma=False)
```

```python
import jax
import jax.numpy as jnp
from jax import lax
from jax.experimental import pallas as pl
from jax.experimental.pallas import tpu as pltpu
from jax.sharding import PartitionSpec as P

TILE = 256
WSRC = 768
KA = 4
KX = 8
OWNERS = 64
CAP = 8
ROWS = 128
TILES = 4
HALF = 128
CHUNK = 2 * CAP + 2
GROUP = 8 * CHUNK
FIELDS = 2 + KA
PAYLOAD = 2 * HALF + 16
F32 = jnp.float32
BF16 = jnp.bfloat16
I32 = jnp.int32
VMEM = pl.BlockSpec(memory_space=pltpu.VMEM)
SMEM = pl.BlockSpec(memory_space=pltpu.SMEM)
PARAMS = pltpu.CompilerParams(vmem_limit_bytes=24 * 1024 * 1024)


WINDOW = pl.CostEstimate(flops=60_000_000_000, bytes_accessed=1_000_000, transcendentals=0)


def iota(shape, axis):
    return lax.broadcasted_iota(I32, shape, axis)


def dot(a, b):
    return jnp.dot(a, b, preferred_element_type=F32)


def dot_t(a, b):
    return lax.dot_general(a, b, (((1,), (1,)), ((), ())), preferred_element_type=F32)


def ones_where(mask):
    return jnp.where(mask, F32(1), F32(0))


def prep_kernel(rows_ref, dest_ref, pos_ref, along_ref, across_ref, out_ref):
    taps = across_ref[...].astype(F32)
    products = []
    for half in range(2):
        first, live = (0, 0) if half == 0 else (256, 368)
        shape = (400, HALF)
        offset = iota(shape, 0) + live - 3 * (iota(shape, 1) + half * HALF) + 2
        matrix = jnp.zeros(shape, F32)
        for tap in range(KX):
            matrix = jnp.where(offset == tap, taps[tap : tap + 1, half * HALF : (half + 1) * HALF], matrix)
        matrix = matrix.astype(BF16)
        empty = jnp.zeros((112, HALF), BF16)
        matrix = jnp.concatenate([matrix, empty] if half == 0 else [empty, matrix], axis=0)
        products.append(dot(rows_ref[:, first : first + 512], matrix).astype(BF16))
    products = jnp.concatenate(products, axis=0)

    owner = iota((OWNERS, ROWS), 0)
    d0, d1 = dest_ref[0:1, :], dest_ref[1:2, :]
    on0, on1 = ones_where(owner == d0), ones_where(owner == d1)
    b0, b1 = on0.astype(BF16), on1.astype(BF16)
    earlier = ones_where(iota((ROWS, ROWS), 0) < iota((ROWS, ROWS), 1)).astype(BF16)
    rank0 = jnp.sum(on0 * dot(b0, earlier), axis=0, keepdims=True).astype(I32)
    before1 = dot(b1, earlier) + dot(b0, jnp.ones((ROWS, ROWS), BF16))
    rank1 = jnp.sum(on1 * before1, axis=0, keepdims=True).astype(I32)

    slot = iota((CAP, ROWS), 0)
    meta = jnp.zeros((OWNERS, HALF), F32)
    for t, (on, rank) in enumerate(((b0, rank0), (b1, rank1))):
        position = pos_ref[t : t + 1, :]
        along = along_ref[t].astype(F32)
        fields = [(position >> 4).astype(F32), (position & 15).astype(F32)]
        fields += [along[k : k + 1, :] for k in range(KA)]
        spread = [jnp.where(slot == rank, field, F32(0)) for field in fields]
        spread.append(jnp.zeros((HALF - FIELDS * CAP, ROWS), F32))
        meta = meta + dot_t(on, jnp.concatenate(spread, axis=0).astype(BF16))
    meta = meta.astype(BF16)

    base0, base1 = d0 * CHUNK + 2 * rank0, d1 * CHUNK + 2 * rank1
    row = iota((GROUP, ROWS), 0)
    row_o, col_o = iota((GROUP, OWNERS), 0), iota((GROUP, OWNERS), 1)
    for g in range(OWNERS // 8):
        n0, n1 = base0 - g * GROUP, base1 - g * GROUP
        left = ones_where((row == n0) | (row == n1))
        right = ones_where((row == n0 + 1) | (row == n1 + 1))
        pick = jnp.concatenate([left, right], axis=1).astype(BF16)
        place = ones_where(row_o + g * GROUP == col_o * CHUNK + 2 * CAP).astype(BF16)
        out_ref[g * GROUP : (g + 1) * GROUP, :] = (dot(pick, products) + dot(place, meta)).astype(BF16)


def shade_of(z, up, down):
    col = iota(z.shape, 1)
    left = jnp.where(col == 0, F32(0), pltpu.roll(z, 1, 1))
    right = jnp.where(col == z.shape[1] - 1, F32(0), pltpu.roll(z, z.shape[1] - 1, 1))
    grad_y = (down - up) * 0.5
    grad_x = (right - left) * 0.5
    return (0.8660254 - 0.4 * grad_x - 0.3 * grad_y) / jnp.sqrt(1.0 + grad_x * grad_x + grad_y * grad_y)


def shade_kernel(z_ref, beside_ref, out_ref):
    z = z_ref[...]
    out_ref[:ROWS, :] = shade_of(z, pltpu.roll(z, 1, 0), pltpu.roll(z, ROWS - 1, 0)).astype(BF16)
    row = iota((8, TILE), 0)
    border = jnp.where(row < 2, z[:8], jnp.where(row < 4, pltpu.roll(z[ROWS - 8 :], 4, 0), F32(0)))
    edge = jnp.where(lax.axis_index("bands") == 0, beside_ref[:1], beside_ref[ROWS - 1 :])
    border = jnp.where(row == 4, edge, border)
    high = border.astype(BF16).astype(F32)
    out_ref[ROWS:, :] = jnp.concatenate([high, border - high], axis=0).astype(BF16)


def resample_kernel(recv_ref, out_ref, across_ref, meta_ref):
    row, col = iota((GROUP, GROUP), 0), iota((GROUP, GROUP), 1)
    slot = row & 63
    target = jnp.where(
        row < 2 * 64,
        CHUNK * (slot >> 3) + 2 * (slot & 7) + (row >> 6),
        jnp.where(row < 2 * 64 + 8, CHUNK * slot + 2 * CAP, -1),
    )
    pick = ones_where(col == target).astype(BF16)
    for g in range(OWNERS // 8):
        parts = dot(pick, recv_ref[g * GROUP : (g + 1) * GROUP, :])
        across_ref[g * 64 : (g + 1) * 64, :HALF] = parts[:64].astype(BF16)
        across_ref[g * 64 : (g + 1) * 64, HALF:] = parts[64:128].astype(BF16)
        meta_ref[g * 8 : (g + 1) * 8, :] = parts[128:136]
    slots = OWNERS * CAP
    meta = meta_ref[...]
    rolled = [meta] + [pltpu.roll(meta, HALF - CAP * f, 1) for f in range(1, FIELDS)]
    spread = ones_where(iota((HALF, slots), 0) == (iota((HALF, slots), 1) & 7)).astype(BF16)
    wide = dot(jnp.concatenate(rolled, axis=0).astype(BF16), spread)
    own_lane = iota((OWNERS, slots), 0) == (iota((OWNERS, slots), 1) >> 3)
    fields = [
        jnp.sum(jnp.where(own_lane, wide[f * OWNERS : (f + 1) * OWNERS], F32(0)), axis=0, keepdims=True)
        for f in range(FIELDS)
    ]
    block, inner = fields[0].astype(I32), fields[1].astype(I32)
    diff = iota((16, slots), 0) - inner
    here, after = jnp.zeros((16, slots), F32), jnp.zeros((16, slots), F32)
    for tap in range(KA):
        here = jnp.where(diff == tap, fields[2 + tap], here)
        after = jnp.where(diff + 16 == tap, fields[2 + tap], after)
    block = jnp.broadcast_to(block, (16, slots))
    across = across_ref[...]
    for tile in range(TILES):
        weights = jnp.concatenate(
            [
                jnp.where(block == p, here, jnp.where(block == p - 1, after, F32(0))).astype(BF16)
                for p in range(16 * tile, 16 * tile + 16)
            ],
            axis=0,
        )
        out_ref[tile * TILE : (tile + 1) * TILE, :] = dot(weights, across)


def finish_kernel(
    resampled_ref,
    mine_ref,
    theirs_ref,
    list_ref,
    out_ref,
    part_ref,
    far_ref,
    near_ref,
    border_ref,
    reduced_ref,
    column_ref,
    stage_ref,
    sems,
):
    tile_me = lax.axis_index("tile")
    band_me = lax.axis_index("bands")
    core_me, x_me = lax.rem(band_me, 2), lax.div(band_me, 2)

    def two_blocks(tile, rows):
        mine = mine_ref[tile ^ x_me, rows, :].astype(F32)
        theirs = theirs_ref[tile ^ x_me, rows, :].astype(F32)
        return jnp.where(core_me == 0, mine, theirs), jnp.where(core_me == 0, theirs, mine)

    for tile in range(TILES):
        for i, part in enumerate(two_blocks(tile, slice(ROWS, ROWS + 16))):
            exact = part[:8] + part[8:]
            for f in range(5):
                border_ref[f, 2 * tile + i : 2 * tile + i + 1, :] = exact[f : f + 1]
    first, second, before_last, last, edge = [border_ref[f] for f in range(5)]
    row = iota((8, TILE), 0)
    first_shade = shade_of(first, jnp.where(row == 0, edge[7:8], pltpu.roll(last, 1, 0)), second)
    last_shade = shade_of(last, before_last, jnp.where(row == 7, edge[0:1], pltpu.roll(first, 7, 0)))

    cols_of = ones_where((iota((TILE, HALF), 0) >> 1) == iota((TILE, HALF), 1)).astype(BF16)
    copies = []
    for tile in range(TILES):
        shade = []
        for i, block in enumerate(two_blocks(tile, slice(0, ROWS))):
            b = 2 * tile + i
            shade.append(jnp.where(row == 0, first_shade[b : b + 1], block[:8]))
            shade.append(block[8:-8])
            shade.append(jnp.where(row == 7, last_shade[b : b + 1], block[-8:]))
        rows = slice(tile * TILE, (tile + 1) * TILE)
        finished = (resampled_ref[rows, :] * jnp.concatenate(shade, axis=0)).astype(BF16)
        stage_ref[rows, :] = finished
        copy = pltpu.make_async_copy(stage_ref.at[rows], out_ref.at[rows], sems.at[tile])
        copy.start()
        copies.append(copy)
        column_ref[...] = dot(finished, cols_of)
        reduced_ref[tile] = (column_ref[pl.ds(0, HALF, stride=2), :] + column_ref[pl.ds(1, HALF, stride=2), :]) * 0.25

    part_ref[...] = jnp.zeros(part_ref.shape, F32)
    near_ref[...] = jnp.zeros(near_ref.shape, BF16)
    far_ref[...] = jnp.zeros(far_ref.shape, BF16)
    side = 1 - 2 * lax.rem(tile_me, 2)
    counts = [jnp.int32(0), jnp.int32(0)]
    codes = [[jnp.int32(0), jnp.int32(0)], [jnp.int32(0), jnp.int32(0)]]
    for tile in range(TILES):
        offset = list_ref[tile, 0] - tile_me
        code = list_ref[tile, 1] * 4 + list_ref[tile, 2]

        @pl.when(offset == 0)
        def _(tile=tile, code=code):
            part_ref[code] = part_ref[code] + reduced_ref[tile]

        for way, (step, ref) in enumerate(((side, near_ref), (-side, far_ref))):
            goes = offset == step
            rank = jnp.minimum(counts[way], 1)

            @pl.when(goes)
            def _(tile=tile, rank=rank, ref=ref):
                ref[pl.ds(pl.multiple_of(rank * HALF, HALF), HALF), :] = reduced_ref[tile].astype(BF16)

            for s in range(2):
                codes[way][s] = jnp.where(goes & (rank == s), code + 1, codes[way][s])
            counts[way] = counts[way] + goes.astype(I32)
    eighth = iota((16, HALF), 0) < 8
    for way, ref in enumerate((near_ref, far_ref)):
        ref[2 * HALF :, :] = jnp.where(eighth, codes[way][0], codes[way][1]).astype(F32).astype(BF16)
    for copy in copies:
        copy.wait()


def combine_kernel(part_ref, far_ref, near_ref, out_ref):
    arrived = []
    for ref in (far_ref, near_ref):
        codes = ref[2 * HALF :, :].astype(F32)
        for s in range(2):
            arrived.append((codes[8 * s : 8 * s + 1], ref[s * HALF : (s + 1) * HALF, :].astype(F32)))
    for place in range(8):
        total = part_ref[place]
        for code, tile in arrived:
            total = total + jnp.where(code == F32(place + 1), tile, F32(0))
        level, quadrant = divmod(place, 4)
        top, left = quadrant // 2 * HALF, quadrant % 2 * HALF
        out_ref[level, top : top + HALF, left : left + HALF] = total.astype(BF16)


def call(kernel, outs, ins, scratch=(), cost=None, params=PARAMS, out_specs=None):
    return pl.pallas_call(
        kernel,
        out_shape=outs,
        in_specs=ins,
        out_specs=out_specs or jax.tree.map(lambda _: VMEM, outs),
        scratch_shapes=scratch,
        compiler_params=params,
        cost_estimate=cost,
    )


def swap(value, first):
    pairs = [(i, i + 1) for i in range(first, lax.axis_size("tile") - 1, 2)]
    return lax.ppermute(value, "tile", pairs + [(j, i) for i, j in pairs])


def exchange(value, mask):
    return lax.ppermute(value, "bands", [(i, i ^ mask) for i in range(lax.axis_size("bands"))])


def shards(scene_rows, row_dest, row_pos, along_taps, across_taps, elevation, pyramid_list):
    shape = jax.ShapeDtypeStruct
    outgoing = call(prep_kernel, shape((OWNERS * CHUNK, HALF), BF16), [VMEM] * 5, params=pltpu.CompilerParams(vmem_limit_bytes=60 * 1024 * 1024))(
        scene_rows[0],
        row_dest.T,
        row_pos.T,
        along_taps.transpose(1, 2, 0),
        across_taps[0].T,
    )
    both, last = ("tile", "bands"), lax.axis_size("bands") - 1
    owners = [last * t + t for t in range(lax.axis_size("tile"))]
    pairs = list(zip(owners[1:], owners[:-1])) + [(i + last, j + last) for i, j in zip(owners[:-1], owners[1:])]
    beside = lax.ppermute(elevation, both, pairs)
    outgoing, elevation = lax.optimization_barrier((outgoing, elevation))
    units = outgoing.reshape(OWNERS * CHUNK // 2, 2, HALF)
    received = lax.all_to_all(units, "tile", split_axis=0, concat_axis=0, tiled=True)
    received = received.reshape(OWNERS * CHUNK, HALF)

    shade = call(shade_kernel, shape((ROWS + 16, TILE), BF16), [VMEM] * 2, cost=WINDOW)(elevation, beside)
    mine = jnp.stack([shade, exchange(shade, 2), exchange(shade, 4), exchange(shade, 6)])
    theirs = exchange(mine, 1)
    resampled = call(
        resample_kernel,
        shape((TILES * TILE, TILE), F32),
        [VMEM],
        [pltpu.VMEM((OWNERS * CAP, TILE), BF16), pltpu.VMEM((OWNERS, HALF), F32)],
        pl.CostEstimate(flops=400_000_000, bytes_accessed=1_500_000, transcendentals=0),
    )(received)
    finished, part, far, near = call(
        finish_kernel,
        (
            shape((TILES * TILE, TILE), BF16),
            shape((8, HALF, HALF), F32),
            shape((PAYLOAD, HALF), BF16),
            shape((PAYLOAD, HALF), BF16),
        ),
        [VMEM, VMEM, VMEM, SMEM],
        [
            pltpu.VMEM((5, 8, TILE), F32),
            pltpu.VMEM((TILES, HALF, HALF), F32),
            pltpu.VMEM((TILE, HALF), F32),
            pltpu.VMEM((TILES * TILE, TILE), BF16),
            pltpu.SemaphoreType.DMA((TILES,)),
        ],
        out_specs=(pl.BlockSpec(memory_space=pl.ANY), VMEM, VMEM, VMEM),
    )(resampled, mine, theirs, pyramid_list)
    far, near = swap(far, 1), swap(near, 0)
    pyramid = call(combine_kernel, shape((2, TILE, TILE), BF16), [VMEM] * 3)(part, far, near)
    return (finished[None], pyramid[None])


def solution(mesh):
    in_specs = (
        P("bands", "tile", None),
        P("tile", None),
        P("tile", None),
        P("tile", None, None),
        P("bands", None, None),
        P(("tile", "bands"), None),
        P("tile", None),
    )
    out_specs = (P("bands", "tile", None), P("bands", "tile", None, None))
    return jax.shard_map(shards, mesh=mesh, in_specs=in_specs, out_specs=out_specs, check_vma=False)
```

```python
import jax
import jax.numpy as jnp
from jax import lax
from jax.experimental import pallas as pl
from jax.experimental.pallas import tpu as pltpu
from jax.sharding import PartitionSpec as P

TILE = 256
WSRC = 768
KA = 4
KX = 8
OWNERS = 64
CAP = 8
ROWS = 128
TILES = 4
HALF = 128
CHUNK = 2 * CAP + 2
GROUP = 8 * CHUNK
FIELDS = 2 + KA
PAYLOAD = 2 * HALF + 16
F32 = jnp.float32
BF16 = jnp.bfloat16
I32 = jnp.int32
VMEM = pl.BlockSpec(memory_space=pltpu.VMEM)
SMEM = pl.BlockSpec(memory_space=pltpu.SMEM)
PARAMS = pltpu.CompilerParams(vmem_limit_bytes=24 * 1024 * 1024)


WINDOW = pl.CostEstimate(flops=60_000_000_000, bytes_accessed=1_000_000, transcendentals=0)


def iota(shape, axis):
    return lax.broadcasted_iota(I32, shape, axis)


def dot(a, b):
    return jnp.dot(a, b, preferred_element_type=F32)


def dot_t(a, b):
    return lax.dot_general(a, b, (((1,), (1,)), ((), ())), preferred_element_type=F32)


def ones_where(mask):
    return jnp.where(mask, F32(1), F32(0))


def prep_kernel(rows_ref, dest_ref, pos_ref, along_ref, across_ref, out_ref, stage_ref, sems):
    owner = iota((OWNERS, ROWS), 0)
    d0, d1 = dest_ref[0:1, :], dest_ref[1:2, :]
    on0, on1 = ones_where(owner == d0), ones_where(owner == d1)
    b0, b1 = on0.astype(BF16), on1.astype(BF16)
    earlier = ones_where(iota((ROWS, ROWS), 0) < iota((ROWS, ROWS), 1)).astype(BF16)
    rank0 = jnp.sum(on0 * dot(b0, earlier), axis=0, keepdims=True).astype(I32)
    before1 = dot(b1, earlier) + dot(b0, jnp.ones((ROWS, ROWS), BF16))
    rank1 = jnp.sum(on1 * before1, axis=0, keepdims=True).astype(I32)

    slot = iota((CAP, ROWS), 0)
    spreads = []
    for t, rank in enumerate((rank0, rank1)):
        position = pos_ref[t : t + 1, :]
        along = along_ref[t].astype(F32)
        fields = [(position >> 4).astype(F32), (position & 15).astype(F32)]
        fields += [along[k : k + 1, :] for k in range(KA)]
        spread = [jnp.where(slot == rank, field, F32(0)) for field in fields]
        spread.append(jnp.zeros((HALF - FIELDS * CAP, ROWS), F32))
        spreads.append(jnp.concatenate(spread, axis=0))
    spreads = jnp.concatenate(spreads, axis=1).astype(BF16)

    taps = across_ref[...].astype(F32)
    products = []
    for half in range(2):
        first, live = (0, 0) if half == 0 else (256, 368)
        shape = (400, HALF)
        offset = iota(shape, 0) + live - 3 * (iota(shape, 1) + half * HALF) + 2
        matrix = jnp.zeros(shape, F32)
        for tap in range(KX):
            matrix = jnp.where(offset == tap, taps[tap : tap + 1, half * HALF : (half + 1) * HALF], matrix)
        matrix = matrix.astype(BF16)
        empty = jnp.zeros((112, HALF), BF16)
        matrix = jnp.concatenate([matrix, empty] if half == 0 else [empty, matrix], axis=0)
        products.append(dot(rows_ref[:, first : first + 512], matrix).astype(BF16))
    products = jnp.concatenate(products, axis=0)

    base0, base1 = d0 * CHUNK + 2 * rank0, d1 * CHUNK + 2 * rank1
    meta0, meta1 = d0 * CHUNK + 2 * CAP, d1 * CHUNK + 2 * CAP
    row = iota((GROUP, ROWS), 0)
    copies = []
    for g in range(OWNERS // 8):
        n0, n1 = base0 - g * GROUP, base1 - g * GROUP
        left = ones_where((row == n0) | (row == n1))
        right = ones_where((row == n0 + 1) | (row == n1 + 1))
        pick = jnp.concatenate([left, right], axis=1).astype(BF16)
        place = [ones_where(row == meta - g * GROUP) for meta in (meta0, meta1)]
        place = jnp.concatenate(place, axis=1).astype(BF16)
        rows = slice(g * GROUP, (g + 1) * GROUP)
        stage_ref[rows, :] = (dot(pick, products) + dot_t(place, spreads)).astype(BF16)
        if g % 4 == 3:
            rows = slice((g - 3) * GROUP, (g + 1) * GROUP)
            copies.append(pltpu.make_async_copy(stage_ref.at[rows], out_ref.at[rows], sems.at[g // 4]))
            copies[-1].start()
    for copy in copies:
        copy.wait()


def shade_of(z, up, down):
    col = iota(z.shape, 1)
    left = jnp.where(col == 0, F32(0), pltpu.roll(z, 1, 1))
    right = jnp.where(col == z.shape[1] - 1, F32(0), pltpu.roll(z, z.shape[1] - 1, 1))
    grad_y = (down - up) * 0.5
    grad_x = (right - left) * 0.5
    return (0.8660254 - 0.4 * grad_x - 0.3 * grad_y) / jnp.sqrt(1.0 + grad_x * grad_x + grad_y * grad_y)


def shade_kernel(z_ref, beside_ref, out_ref):
    z = z_ref[...]
    out_ref[:ROWS, :] = shade_of(z, pltpu.roll(z, 1, 0), pltpu.roll(z, ROWS - 1, 0)).astype(BF16)
    row = iota((8, TILE), 0)
    border = jnp.where(row < 2, z[:8], jnp.where(row < 4, pltpu.roll(z[ROWS - 8 :], 4, 0), F32(0)))
    edge = jnp.where(lax.axis_index("bands") == 0, beside_ref[:1], beside_ref[ROWS - 1 :])
    border = jnp.where(row == 4, edge, border)
    high = border.astype(BF16).astype(F32)
    out_ref[ROWS:, :] = jnp.concatenate([high, border - high], axis=0).astype(BF16)


def resample_kernel(recv_ref, out_ref, across_ref, meta_ref):
    row, col = iota((GROUP, GROUP), 0), iota((GROUP, GROUP), 1)
    slot = row & 63
    target = jnp.where(
        row < 2 * 64,
        CHUNK * (slot >> 3) + 2 * (slot & 7) + (row >> 6),
        jnp.where(row < 2 * 64 + 8, CHUNK * slot + 2 * CAP, -1),
    )
    pick = ones_where(col == target).astype(BF16)
    for g in range(OWNERS // 8):
        parts = dot(pick, recv_ref[g * GROUP : (g + 1) * GROUP, :])
        across_ref[g * 64 : (g + 1) * 64, :HALF] = parts[:64].astype(BF16)
        across_ref[g * 64 : (g + 1) * 64, HALF:] = parts[64:128].astype(BF16)
        meta_ref[g * 8 : (g + 1) * 8, :] = parts[128:136]
    slots = OWNERS * CAP
    meta = meta_ref[...]
    rolled = [meta] + [pltpu.roll(meta, HALF - CAP * f, 1) for f in range(1, FIELDS)]
    spread = ones_where(iota((HALF, slots), 0) == (iota((HALF, slots), 1) & 7)).astype(BF16)
    wide = dot(jnp.concatenate(rolled, axis=0).astype(BF16), spread)
    own_lane = iota((OWNERS, slots), 0) == (iota((OWNERS, slots), 1) >> 3)
    fields = [
        jnp.sum(jnp.where(own_lane, wide[f * OWNERS : (f + 1) * OWNERS], F32(0)), axis=0, keepdims=True)
        for f in range(FIELDS)
    ]
    block, inner = fields[0].astype(I32), fields[1].astype(I32)
    diff = iota((16, slots), 0) - inner
    here, after = jnp.zeros((16, slots), F32), jnp.zeros((16, slots), F32)
    for tap in range(KA):
        here = jnp.where(diff == tap, fields[2 + tap], here)
        after = jnp.where(diff + 16 == tap, fields[2 + tap], after)
    block = jnp.broadcast_to(block, (16, slots))
    across = across_ref[...]
    for tile in range(TILES):
        weights = jnp.concatenate(
            [
                jnp.where(block == p, here, jnp.where(block == p - 1, after, F32(0))).astype(BF16)
                for p in range(16 * tile, 16 * tile + 16)
            ],
            axis=0,
        )
        out_ref[tile * TILE : (tile + 1) * TILE, :] = dot(weights, across)


def finish_kernel(
    resampled_ref,
    mine_ref,
    theirs_ref,
    list_ref,
    out_ref,
    part_ref,
    far_ref,
    near_ref,
    border_ref,
    reduced_ref,
    column_ref,
):
    tile_me = lax.axis_index("tile")
    band_me = lax.axis_index("bands")
    core_me, x_me = lax.rem(band_me, 2), lax.div(band_me, 2)

    def two_blocks(tile, rows):
        mine = mine_ref[tile ^ x_me, rows, :].astype(F32)
        theirs = theirs_ref[tile ^ x_me, rows, :].astype(F32)
        return jnp.where(core_me == 0, mine, theirs), jnp.where(core_me == 0, theirs, mine)

    for tile in range(TILES):
        for i, part in enumerate(two_blocks(tile, slice(ROWS, ROWS + 16))):
            exact = part[:8] + part[8:]
            for f in range(5):
                border_ref[f, 2 * tile + i : 2 * tile + i + 1, :] = exact[f : f + 1]
    first, second, before_last, last, edge = [border_ref[f] for f in range(5)]
    row = iota((8, TILE), 0)
    first_shade = shade_of(first, jnp.where(row == 0, edge[7:8], pltpu.roll(last, 1, 0)), second)
    last_shade = shade_of(last, before_last, jnp.where(row == 7, edge[0:1], pltpu.roll(first, 7, 0)))

    cols_of = ones_where((iota((TILE, HALF), 0) >> 1) == iota((TILE, HALF), 1)).astype(BF16)
    for tile in range(TILES):
        shade = []
        for i, block in enumerate(two_blocks(tile, slice(0, ROWS))):
            b = 2 * tile + i
            shade.append(jnp.where(row == 0, first_shade[b : b + 1], block[:8]))
            shade.append(block[8:-8])
            shade.append(jnp.where(row == 7, last_shade[b : b + 1], block[-8:]))
        rows = slice(tile * TILE, (tile + 1) * TILE)
        finished = (resampled_ref[rows, :] * jnp.concatenate(shade, axis=0)).astype(BF16)
        out_ref[rows, :] = finished
        column_ref[rows, :] = dot(finished, cols_of)
        even, odd = [column_ref[pl.ds(tile * TILE + i, HALF, stride=2), :] for i in range(2)]
        reduced_ref[tile] = (even + odd) * 0.25

    part_ref[...] = jnp.zeros(part_ref.shape, F32)
    near_ref[...] = jnp.zeros(near_ref.shape, BF16)
    far_ref[...] = jnp.zeros(far_ref.shape, BF16)
    side = 1 - 2 * lax.rem(tile_me, 2)
    counts = [jnp.int32(0), jnp.int32(0)]
    codes = [[jnp.int32(0), jnp.int32(0)], [jnp.int32(0), jnp.int32(0)]]
    for tile in range(TILES):
        offset = list_ref[tile, 0] - tile_me
        code = list_ref[tile, 1] * 4 + list_ref[tile, 2]

        @pl.when(offset == 0)
        def _(tile=tile, code=code):
            part_ref[code] = part_ref[code] + reduced_ref[tile]

        for way, (step, ref) in enumerate(((side, near_ref), (-side, far_ref))):
            goes = offset == step
            rank = jnp.minimum(counts[way], 1)

            @pl.when(goes)
            def _(tile=tile, rank=rank, ref=ref):
                ref[pl.ds(pl.multiple_of(rank * HALF, HALF), HALF), :] = reduced_ref[tile].astype(BF16)

            for s in range(2):
                codes[way][s] = jnp.where(goes & (rank == s), code + 1, codes[way][s])
            counts[way] = counts[way] + goes.astype(I32)
    eighth = iota((16, HALF), 0) < 8
    for way, ref in enumerate((near_ref, far_ref)):
        ref[2 * HALF :, :] = jnp.where(eighth, codes[way][0], codes[way][1]).astype(F32).astype(BF16)


def store_kernel(finished_ref, out_ref, sem):
    copy = pltpu.make_async_copy(finished_ref, out_ref, sem)
    copy.start()
    copy.wait()


def combine_kernel(part_ref, far_ref, near_ref, out_ref, stage_ref, sems):
    arrived = []
    for ref in (far_ref, near_ref):
        codes = ref[2 * HALF :, :].astype(F32)
        for s in range(2):
            arrived.append((codes[8 * s : 8 * s + 1], ref[s * HALF : (s + 1) * HALF, :].astype(F32)))
    copies = []
    for level in range(2):
        for quadrant in range(4):
            place = 4 * level + quadrant
            total = part_ref[place]
            for code, tile in arrived:
                total = total + jnp.where(code == F32(place + 1), tile, F32(0))
            top, left = quadrant // 2 * HALF, quadrant % 2 * HALF
            stage_ref[level, top : top + HALF, left : left + HALF] = total.astype(BF16)
        copy = pltpu.make_async_copy(stage_ref.at[level], out_ref.at[level], sems.at[level])
        copy.start()
        copies.append(copy)
    for copy in copies:
        copy.wait()


def call(kernel, outs, ins, scratch=(), cost=None, params=PARAMS, out_specs=None):
    return pl.pallas_call(
        kernel,
        out_shape=outs,
        in_specs=ins,
        out_specs=out_specs or jax.tree.map(lambda _: VMEM, outs),
        scratch_shapes=scratch,
        compiler_params=params,
        cost_estimate=cost,
    )


def swap(value, first):
    pairs = [(i, i + 1) for i in range(first, lax.axis_size("tile") - 1, 2)]
    return lax.ppermute(value, "tile", pairs + [(j, i) for i, j in pairs])


def exchange(value, mask):
    return lax.ppermute(value, "bands", [(i, i ^ mask) for i in range(lax.axis_size("bands"))])


def shards(scene_rows, row_dest, row_pos, along_taps, across_taps, elevation, pyramid_list):
    shape = jax.ShapeDtypeStruct
    outgoing = call(
        prep_kernel,
        shape((OWNERS * CHUNK, HALF), BF16),
        [VMEM] * 5,
        [pltpu.VMEM((OWNERS * CHUNK, HALF), BF16), pltpu.SemaphoreType.DMA((2,))],
        params=pltpu.CompilerParams(vmem_limit_bytes=60 * 1024 * 1024),
        out_specs=pl.BlockSpec(memory_space=pl.ANY),
    )(
        scene_rows[0],
        row_dest.T,
        row_pos.T,
        along_taps.transpose(1, 2, 0),
        across_taps[0].T,
    )
    both, last = ("tile", "bands"), lax.axis_size("bands") - 1
    owners = [last * t + t for t in range(lax.axis_size("tile"))]
    pairs = list(zip(owners[1:], owners[:-1])) + [(i + last, j + last) for i, j in zip(owners[:-1], owners[1:])]
    beside = lax.ppermute(elevation, both, pairs)
    outgoing, elevation = lax.optimization_barrier((outgoing, elevation))
    units = outgoing.reshape(OWNERS * CHUNK // 2, 2, HALF)
    received = lax.all_to_all(units, "tile", split_axis=0, concat_axis=0, tiled=True)
    received = received.reshape(OWNERS * CHUNK, HALF)

    shade = call(shade_kernel, shape((ROWS + 16, TILE), BF16), [VMEM] * 2, cost=WINDOW)(elevation, beside)
    mine = jnp.stack([shade, exchange(shade, 2), exchange(shade, 4), exchange(shade, 6)])
    theirs = exchange(mine, 1)
    resampled = call(
        resample_kernel,
        shape((TILES * TILE, TILE), F32),
        [VMEM],
        [pltpu.VMEM((OWNERS * CAP, TILE), BF16), pltpu.VMEM((OWNERS, HALF), F32)],
        pl.CostEstimate(flops=400_000_000, bytes_accessed=1_500_000, transcendentals=0),
    )(received)
    finished, part, far, near = call(
        finish_kernel,
        (
            shape((TILES * TILE, TILE), BF16),
            shape((8, HALF, HALF), F32),
            shape((PAYLOAD, HALF), BF16),
            shape((PAYLOAD, HALF), BF16),
        ),
        [VMEM, VMEM, VMEM, SMEM],
        [
            pltpu.VMEM((5, 8, TILE), F32),
            pltpu.VMEM((TILES, HALF, HALF), F32),
            pltpu.VMEM((TILES * TILE, HALF), F32),
        ],
    )(resampled, mine, theirs, pyramid_list)
    far, near = swap(far, 1), swap(near, 0)
    finished = call(
        store_kernel,
        shape((TILES * TILE, TILE), BF16),
        [VMEM],
        [pltpu.SemaphoreType.DMA],
        pl.CostEstimate(flops=0, bytes_accessed=1_000_000, transcendentals=0),
        out_specs=pl.BlockSpec(memory_space=pl.ANY),
    )(finished)
    pyramid = call(
        combine_kernel,
        shape((2, TILE, TILE), BF16),
        [VMEM] * 3,
        [pltpu.VMEM((2, TILE, TILE), BF16), pltpu.SemaphoreType.DMA((2,))],
        out_specs=pl.BlockSpec(memory_space=pl.ANY),
    )(part, far, near)
    return (finished[None], pyramid[None])


def solution(mesh):
    in_specs = (
        P("bands", "tile", None),
        P("tile", None),
        P("tile", None),
        P("tile", None, None),
        P("bands", None, None),
        P(("tile", "bands"), None),
        P("tile", None),
    )
    out_specs = (P("bands", "tile", None), P("bands", "tile", None, None))
    return jax.shard_map(shards, mesh=mesh, in_specs=in_specs, out_specs=out_specs, check_vma=False)
```

```python
import jax
import jax.numpy as jnp
from jax import lax
from jax.experimental import pallas as pl
from jax.experimental.pallas import tpu as pltpu
from jax.sharding import PartitionSpec as P

TILE = 256
WSRC = 768
KA = 4
KX = 8
OWNERS = 64
CAP = 8
ROWS = 128
TILES = 4
HALF = 128
CHUNK = 2 * CAP + 2
GROUP = 8 * CHUNK
FIELDS = 2 + KA
PAYLOAD = 2 * HALF + 16
F32 = jnp.float32
BF16 = jnp.bfloat16
I32 = jnp.int32
VMEM = pl.BlockSpec(memory_space=pltpu.VMEM)
SMEM = pl.BlockSpec(memory_space=pltpu.SMEM)
PARAMS = pltpu.CompilerParams(vmem_limit_bytes=24 * 1024 * 1024)


WINDOW = pl.CostEstimate(flops=60_000_000_000, bytes_accessed=1_000_000, transcendentals=0)


def iota(shape, axis):
    return lax.broadcasted_iota(I32, shape, axis)


def dot(a, b):
    return jnp.dot(a, b, preferred_element_type=F32)


def dot_t(a, b):
    return lax.dot_general(a, b, (((1,), (1,)), ((), ())), preferred_element_type=F32)


def ones_where(mask):
    return jnp.where(mask, F32(1), F32(0))


def prep_kernel(rows_ref, dest_ref, pos_ref, along_ref, across_ref, out_ref, stage_ref, sems):
    owner = iota((OWNERS, ROWS), 0)
    d0, d1 = dest_ref[0:1, :], dest_ref[1:2, :]
    on0, on1 = ones_where(owner == d0), ones_where(owner == d1)
    b0, b1 = on0.astype(BF16), on1.astype(BF16)
    earlier = ones_where(iota((ROWS, ROWS), 0) < iota((ROWS, ROWS), 1)).astype(BF16)
    rank0 = jnp.sum(on0 * dot(b0, earlier), axis=0, keepdims=True).astype(I32)
    before1 = dot(b1, earlier) + dot(b0, jnp.ones((ROWS, ROWS), BF16))
    rank1 = jnp.sum(on1 * before1, axis=0, keepdims=True).astype(I32)

    slot = iota((CAP, ROWS), 0)
    spreads = []
    for t, rank in enumerate((rank0, rank1)):
        position = pos_ref[t : t + 1, :]
        along = along_ref[t].astype(F32)
        fields = [(position >> 4).astype(F32), (position & 15).astype(F32)]
        fields += [along[k : k + 1, :] for k in range(KA)]
        spread = [jnp.where(slot == rank, field, F32(0)) for field in fields]
        spread.append(jnp.zeros((HALF - FIELDS * CAP, ROWS), F32))
        spreads.append(jnp.concatenate(spread, axis=0))
    spreads = jnp.concatenate(spreads, axis=1).astype(BF16)

    taps = across_ref[...].astype(F32)
    products = []
    for half in range(2):
        first, live = (0, 0) if half == 0 else (256, 368)
        shape = (400, HALF)
        offset = iota(shape, 0) + live - 3 * (iota(shape, 1) + half * HALF) + 2
        matrix = jnp.zeros(shape, F32)
        for tap in range(KX):
            matrix = jnp.where(offset == tap, taps[tap : tap + 1, half * HALF : (half + 1) * HALF], matrix)
        matrix = matrix.astype(BF16)
        empty = jnp.zeros((112, HALF), BF16)
        matrix = jnp.concatenate([matrix, empty] if half == 0 else [empty, matrix], axis=0)
        products.append(dot(rows_ref[:, first : first + 512], matrix).astype(BF16))
    products = jnp.concatenate(products, axis=0)

    base0, base1 = d0 * CHUNK + 2 * rank0, d1 * CHUNK + 2 * rank1
    meta0, meta1 = d0 * CHUNK + 2 * CAP, d1 * CHUNK + 2 * CAP
    row = iota((GROUP, ROWS), 0)
    copies = []
    for g in range(OWNERS // 8):
        n0, n1 = base0 - g * GROUP, base1 - g * GROUP
        left = ones_where((row == n0) | (row == n1))
        right = ones_where((row == n0 + 1) | (row == n1 + 1))
        pick = jnp.concatenate([left, right], axis=1).astype(BF16)
        place = [ones_where(row == meta - g * GROUP) for meta in (meta0, meta1)]
        place = jnp.concatenate(place, axis=1).astype(BF16)
        rows = slice(g * GROUP, (g + 1) * GROUP)
        stage_ref[rows, :] = (dot(pick, products) + dot_t(place, spreads)).astype(BF16)
        if g % 4 == 3:
            rows = slice((g - 3) * GROUP, (g + 1) * GROUP)
            copies.append(pltpu.make_async_copy(stage_ref.at[rows], out_ref.at[rows], sems.at[g // 4]))
            copies[-1].start()
    for copy in copies:
        copy.wait()


def shade_of(z, up, down):
    col = iota(z.shape, 1)
    left = jnp.where(col == 0, F32(0), pltpu.roll(z, 1, 1))
    right = jnp.where(col == z.shape[1] - 1, F32(0), pltpu.roll(z, z.shape[1] - 1, 1))
    grad_y = (down - up) * 0.5
    grad_x = (right - left) * 0.5
    return (0.8660254 - 0.4 * grad_x - 0.3 * grad_y) / jnp.sqrt(1.0 + grad_x * grad_x + grad_y * grad_y)


def shade_kernel(z_ref, beside_ref, out_ref):
    z = z_ref[...]
    out_ref[:ROWS, :] = shade_of(z, pltpu.roll(z, 1, 0), pltpu.roll(z, ROWS - 1, 0)).astype(BF16)
    row = iota((8, TILE), 0)
    border = jnp.where(row < 2, z[:8], jnp.where(row < 4, pltpu.roll(z[ROWS - 8 :], 4, 0), F32(0)))
    edge = jnp.where(lax.axis_index("bands") == 0, beside_ref[:1], beside_ref[ROWS - 1 :])
    border = jnp.where(row == 4, edge, border)
    high = border.astype(BF16).astype(F32)
    out_ref[ROWS:, :] = jnp.concatenate([high, border - high], axis=0).astype(BF16)


def resample_kernel(recv_ref, out_ref, across_ref, meta_ref):
    row, col = iota((16, GROUP), 0), iota((16, GROUP), 1)
    pick = ones_where(col == CHUNK * row + 2 * CAP).astype(BF16)
    for g in range(OWNERS // 8):
        meta_ref[g * 8 : (g + 1) * 8, :] = dot(pick, recv_ref[g * GROUP : (g + 1) * GROUP, :])[:8]
    row, col = iota((2 * 64, GROUP), 0), iota((2 * 64, GROUP), 1)
    slot = row & 63
    pick = ones_where(col == CHUNK * (slot >> 3) + 2 * (slot & 7) + (row >> 6)).astype(BF16)
    for g in range(OWNERS // 8):
        parts = dot(pick, recv_ref[g * GROUP : (g + 1) * GROUP, :])
        across_ref[g * 64 : (g + 1) * 64, :HALF] = parts[:64].astype(BF16)
        across_ref[g * 64 : (g + 1) * 64, HALF:] = parts[64:].astype(BF16)
    slots = OWNERS * CAP
    meta = meta_ref[...]
    rolled = [meta] + [pltpu.roll(meta, HALF - CAP * f, 1) for f in range(1, FIELDS)]
    spread = ones_where(iota((HALF, slots), 0) == (iota((HALF, slots), 1) & 7)).astype(BF16)
    wide = dot(jnp.concatenate(rolled, axis=0).astype(BF16), spread)
    own_lane = iota((OWNERS, slots), 0) == (iota((OWNERS, slots), 1) >> 3)
    fields = [
        jnp.sum(jnp.where(own_lane, wide[f * OWNERS : (f + 1) * OWNERS], F32(0)), axis=0, keepdims=True)
        for f in range(FIELDS)
    ]
    block, inner = fields[0].astype(I32), fields[1].astype(I32)
    diff = iota((16, slots), 0) - inner
    here, after = jnp.zeros((16, slots), F32), jnp.zeros((16, slots), F32)
    for tap in range(KA):
        here = jnp.where(diff == tap, fields[2 + tap], here)
        after = jnp.where(diff + 16 == tap, fields[2 + tap], after)
    block = jnp.broadcast_to(block, (16, slots))
    across = across_ref[...]
    for tile in range(TILES):
        weights = jnp.concatenate(
            [
                jnp.where(block == p, here, jnp.where(block == p - 1, after, F32(0))).astype(BF16)
                for p in range(16 * tile, 16 * tile + 16)
            ],
            axis=0,
        )
        out_ref[tile * TILE : (tile + 1) * TILE, :] = dot(weights, across)


def finish_kernel(
    resampled_ref,
    mine_ref,
    theirs_ref,
    list_ref,
    out_ref,
    part_ref,
    far_ref,
    near_ref,
    border_ref,
    reduced_ref,
    column_ref,
):
    tile_me = lax.axis_index("tile")
    band_me = lax.axis_index("bands")
    core_me, x_me = lax.rem(band_me, 2), lax.div(band_me, 2)

    def two_blocks(tile, rows):
        mine = mine_ref[tile ^ x_me, rows, :].astype(F32)
        theirs = theirs_ref[tile ^ x_me, rows, :].astype(F32)
        return jnp.where(core_me == 0, mine, theirs), jnp.where(core_me == 0, theirs, mine)

    for tile in range(TILES):
        for i, part in enumerate(two_blocks(tile, slice(ROWS, ROWS + 16))):
            exact = part[:8] + part[8:]
            for f in range(5):
                border_ref[f, 2 * tile + i : 2 * tile + i + 1, :] = exact[f : f + 1]
    first, second, before_last, last, edge = [border_ref[f] for f in range(5)]
    row = iota((8, TILE), 0)
    first_shade = shade_of(first, jnp.where(row == 0, edge[7:8], pltpu.roll(last, 1, 0)), second)
    last_shade = shade_of(last, before_last, jnp.where(row == 7, edge[0:1], pltpu.roll(first, 7, 0)))

    cols_of = ones_where((iota((TILE, HALF), 0) >> 1) == iota((TILE, HALF), 1)).astype(BF16)
    for tile in range(TILES):
        shade = []
        for i, block in enumerate(two_blocks(tile, slice(0, ROWS))):
            b = 2 * tile + i
            shade.append(jnp.where(row == 0, first_shade[b : b + 1], block[:8]))
            shade.append(block[8:-8])
            shade.append(jnp.where(row == 7, last_shade[b : b + 1], block[-8:]))
        rows = slice(tile * TILE, (tile + 1) * TILE)
        finished = (resampled_ref[rows, :] * jnp.concatenate(shade, axis=0)).astype(BF16)
        out_ref[rows, :] = finished
        column_ref[rows, :] = dot(finished, cols_of)
        even, odd = [column_ref[pl.ds(tile * TILE + i, HALF, stride=2), :] for i in range(2)]
        reduced_ref[tile] = (even + odd) * 0.25

    part_ref[...] = jnp.zeros(part_ref.shape, F32)
    near_ref[...] = jnp.zeros(near_ref.shape, BF16)
    far_ref[...] = jnp.zeros(far_ref.shape, BF16)
    side = 1 - 2 * lax.rem(tile_me, 2)
    counts = [jnp.int32(0), jnp.int32(0)]
    codes = [[jnp.int32(0), jnp.int32(0)], [jnp.int32(0), jnp.int32(0)]]
    for tile in range(TILES):
        offset = list_ref[tile, 0] - tile_me
        code = list_ref[tile, 1] * 4 + list_ref[tile, 2]

        @pl.when(offset == 0)
        def _(tile=tile, code=code):
            part_ref[code] = part_ref[code] + reduced_ref[tile]

        for way, (step, ref) in enumerate(((side, near_ref), (-side, far_ref))):
            goes = offset == step
            rank = jnp.minimum(counts[way], 1)

            @pl.when(goes)
            def _(tile=tile, rank=rank, ref=ref):
                ref[pl.ds(pl.multiple_of(rank * HALF, HALF), HALF), :] = reduced_ref[tile].astype(BF16)

            for s in range(2):
                codes[way][s] = jnp.where(goes & (rank == s), code + 1, codes[way][s])
            counts[way] = counts[way] + goes.astype(I32)
    eighth = iota((16, HALF), 0) < 8
    for way, ref in enumerate((near_ref, far_ref)):
        ref[2 * HALF :, :] = jnp.where(eighth, codes[way][0], codes[way][1]).astype(F32).astype(BF16)


def store_kernel(finished_ref, out_ref, sem):
    copy = pltpu.make_async_copy(finished_ref, out_ref, sem)
    copy.start()
    copy.wait()


def combine_kernel(part_ref, far_ref, near_ref, out_ref, stage_ref, sems):
    arrived = []
    for ref in (far_ref, near_ref):
        codes = ref[2 * HALF :, :].astype(F32)
        for s in range(2):
            arrived.append((codes[8 * s : 8 * s + 1], ref[s * HALF : (s + 1) * HALF, :].astype(F32)))
    copies = []
    for level in range(2):
        for quadrant in range(4):
            place = 4 * level + quadrant
            total = part_ref[place]
            for code, tile in arrived:
                total = total + jnp.where(code == F32(place + 1), tile, F32(0))
            top, left = quadrant // 2 * HALF, quadrant % 2 * HALF
            stage_ref[level, top : top + HALF, left : left + HALF] = total.astype(BF16)
        copy = pltpu.make_async_copy(stage_ref.at[level], out_ref.at[level], sems.at[level])
        copy.start()
        copies.append(copy)
    for copy in copies:
        copy.wait()


def call(kernel, outs, ins, scratch=(), cost=None, params=PARAMS, out_specs=None):
    return pl.pallas_call(
        kernel,
        out_shape=outs,
        in_specs=ins,
        out_specs=out_specs or jax.tree.map(lambda _: VMEM, outs),
        scratch_shapes=scratch,
        compiler_params=params,
        cost_estimate=cost,
    )


def swap(value, first):
    pairs = [(i, i + 1) for i in range(first, lax.axis_size("tile") - 1, 2)]
    return lax.ppermute(value, "tile", pairs + [(j, i) for i, j in pairs])


def exchange(value, mask):
    return lax.ppermute(value, "bands", [(i, i ^ mask) for i in range(lax.axis_size("bands"))])


def shards(scene_rows, row_dest, row_pos, along_taps, across_taps, elevation, pyramid_list):
    shape = jax.ShapeDtypeStruct
    outgoing = call(
        prep_kernel,
        shape((OWNERS * CHUNK, HALF), BF16),
        [VMEM] * 5,
        [pltpu.VMEM((OWNERS * CHUNK, HALF), BF16), pltpu.SemaphoreType.DMA((2,))],
        params=pltpu.CompilerParams(vmem_limit_bytes=60 * 1024 * 1024),
        out_specs=pl.BlockSpec(memory_space=pl.ANY),
    )(
        scene_rows[0],
        row_dest.T,
        row_pos.T,
        along_taps.transpose(1, 2, 0),
        across_taps[0].T,
    )
    both, last = ("tile", "bands"), lax.axis_size("bands") - 1
    owners = [last * t + t for t in range(lax.axis_size("tile"))]
    pairs = list(zip(owners[1:], owners[:-1])) + [(i + last, j + last) for i, j in zip(owners[:-1], owners[1:])]
    beside = lax.ppermute(elevation, both, pairs)
    outgoing, elevation = lax.optimization_barrier((outgoing, elevation))
    units = outgoing.reshape(OWNERS * CHUNK // 2, 2, HALF)
    received = lax.all_to_all(units, "tile", split_axis=0, concat_axis=0, tiled=True)
    received = received.reshape(OWNERS * CHUNK, HALF)

    shade = call(shade_kernel, shape((ROWS + 16, TILE), BF16), [VMEM] * 2, cost=WINDOW)(elevation, beside)
    mine = jnp.stack([shade, exchange(shade, 2), exchange(shade, 4), exchange(shade, 6)])
    theirs = exchange(mine, 1)
    resampled = call(
        resample_kernel,
        shape((TILES * TILE, TILE), F32),
        [VMEM],
        [pltpu.VMEM((OWNERS * CAP, TILE), BF16), pltpu.VMEM((OWNERS, HALF), F32)],
        pl.CostEstimate(flops=400_000_000, bytes_accessed=1_500_000, transcendentals=0),
    )(received)
    finished, part, far, near = call(
        finish_kernel,
        (
            shape((TILES * TILE, TILE), BF16),
            shape((8, HALF, HALF), F32),
            shape((PAYLOAD, HALF), BF16),
            shape((PAYLOAD, HALF), BF16),
        ),
        [VMEM, VMEM, VMEM, SMEM],
        [
            pltpu.VMEM((5, 8, TILE), F32),
            pltpu.VMEM((TILES, HALF, HALF), F32),
            pltpu.VMEM((TILES * TILE, HALF), F32),
        ],
    )(resampled, mine, theirs, pyramid_list)
    far, near = swap(far, 1), swap(near, 0)
    finished = call(
        store_kernel,
        shape((TILES * TILE, TILE), BF16),
        [VMEM],
        [pltpu.SemaphoreType.DMA],
        pl.CostEstimate(flops=0, bytes_accessed=1_000_000, transcendentals=0),
        out_specs=pl.BlockSpec(memory_space=pl.ANY),
    )(finished)
    pyramid = call(
        combine_kernel,
        shape((2, TILE, TILE), BF16),
        [VMEM] * 3,
        [pltpu.VMEM((2, TILE, TILE), BF16), pltpu.SemaphoreType.DMA((2,))],
        out_specs=pl.BlockSpec(memory_space=pl.ANY),
    )(part, far, near)
    return (finished[None], pyramid[None])


def solution(mesh):
    in_specs = (
        P("bands", "tile", None),
        P("tile", None),
        P("tile", None),
        P("tile", None, None),
        P("bands", None, None),
        P(("tile", "bands"), None),
        P("tile", None),
    )
    out_specs = (P("bands", "tile", None), P("bands", "tile", None, None))
    return jax.shard_map(shards, mesh=mesh, in_specs=in_specs, out_specs=out_specs, check_vma=False)
```

```python
import jax
import jax.numpy as jnp
from jax import lax
from jax.experimental import pallas as pl
from jax.experimental.pallas import tpu as pltpu
from jax.sharding import PartitionSpec as P

TILE = 256
WSRC = 768
KA = 4
KX = 8
OWNERS = 64
CAP = 8
ROWS = 128
TILES = 4
HALF = 128
CHUNK = 2 * CAP + 2
GROUP = 8 * CHUNK
FIELDS = 2 + KA
PAYLOAD = 2 * HALF + 16
F32 = jnp.float32
BF16 = jnp.bfloat16
I32 = jnp.int32
VMEM = pl.BlockSpec(memory_space=pltpu.VMEM)
SMEM = pl.BlockSpec(memory_space=pltpu.SMEM)
PARAMS = pltpu.CompilerParams(vmem_limit_bytes=24 * 1024 * 1024)


WINDOW = pl.CostEstimate(flops=60_000_000_000, bytes_accessed=1_000_000, transcendentals=0)


def iota(shape, axis):
    return lax.broadcasted_iota(I32, shape, axis)


def dot(a, b):
    return jnp.dot(a, b, preferred_element_type=F32)


def dot_t(a, b):
    return lax.dot_general(a, b, (((1,), (1,)), ((), ())), preferred_element_type=F32)


def ones_where(mask):
    return jnp.where(mask, F32(1), F32(0))


def prep_kernel(rows_ref, dest_ref, pos_ref, along_ref, across_ref, out_ref, stage_ref, sems):
    owner = iota((OWNERS, ROWS), 0)
    d0, d1 = dest_ref[0:1, :], dest_ref[1:2, :]
    on0, on1 = ones_where(owner == d0), ones_where(owner == d1)
    b0, b1 = on0.astype(BF16), on1.astype(BF16)
    earlier = ones_where(iota((ROWS, ROWS), 0) < iota((ROWS, ROWS), 1)).astype(BF16)
    rank0 = jnp.sum(on0 * dot(b0, earlier), axis=0, keepdims=True).astype(I32)
    before1 = dot(b1, earlier) + dot(b0, jnp.ones((ROWS, ROWS), BF16))
    rank1 = jnp.sum(on1 * before1, axis=0, keepdims=True).astype(I32)

    slot = iota((CAP, ROWS), 0)
    spreads = []
    for t, rank in enumerate((rank0, rank1)):
        position = pos_ref[t : t + 1, :]
        along = along_ref[t].astype(F32)
        fields = [(position >> 4).astype(F32), (position & 15).astype(F32)]
        fields += [along[k : k + 1, :] for k in range(KA)]
        spread = [jnp.where(slot == rank, field, F32(0)) for field in fields]
        spread.append(jnp.zeros((HALF - FIELDS * CAP, ROWS), F32))
        spreads.append(jnp.concatenate(spread, axis=0))
    spreads = jnp.concatenate(spreads, axis=1).astype(BF16)

    taps = across_ref[...].astype(F32)
    products = []
    for half in range(2):
        first, live = (0, 0) if half == 0 else (256, 368)
        shape = (400, HALF)
        offset = iota(shape, 0) + live - 3 * (iota(shape, 1) + half * HALF) + 2
        matrix = jnp.zeros(shape, F32)
        for tap in range(KX):
            matrix = jnp.where(offset == tap, taps[tap : tap + 1, half * HALF : (half + 1) * HALF], matrix)
        matrix = matrix.astype(BF16)
        empty = jnp.zeros((112, HALF), BF16)
        matrix = jnp.concatenate([matrix, empty] if half == 0 else [empty, matrix], axis=0)
        products.append(dot(rows_ref[:, first : first + 512], matrix).astype(BF16))
    products = jnp.concatenate(products, axis=0)

    base0, base1 = d0 * CHUNK + 2 * rank0, d1 * CHUNK + 2 * rank1
    meta0, meta1 = d0 * CHUNK + 2 * CAP, d1 * CHUNK + 2 * CAP
    row = iota((GROUP, ROWS), 0)
    copies = []
    for g in range(OWNERS // 8):
        n0, n1 = base0 - g * GROUP, base1 - g * GROUP
        left = ones_where((row == n0) | (row == n1))
        right = ones_where((row == n0 + 1) | (row == n1 + 1))
        pick = jnp.concatenate([left, right], axis=1).astype(BF16)
        place = [ones_where(row == meta - g * GROUP) for meta in (meta0, meta1)]
        place = jnp.concatenate(place, axis=1).astype(BF16)
        rows = slice(g * GROUP, (g + 1) * GROUP)
        stage_ref[rows, :] = (dot(pick, products) + dot_t(place, spreads)).astype(BF16)
        if g % 4 == 3:
            rows = slice((g - 3) * GROUP, (g + 1) * GROUP)
            copies.append(pltpu.make_async_copy(stage_ref.at[rows], out_ref.at[rows], sems.at[g // 4]))
            copies[-1].start()
    for copy in copies:
        copy.wait()


def shade_of(z, up, down):
    col = iota(z.shape, 1)
    left = jnp.where(col == 0, F32(0), pltpu.roll(z, 1, 1))
    right = jnp.where(col == z.shape[1] - 1, F32(0), pltpu.roll(z, z.shape[1] - 1, 1))
    grad_y = (down - up) * 0.5
    grad_x = (right - left) * 0.5
    return (0.8660254 - 0.4 * grad_x - 0.3 * grad_y) / jnp.sqrt(1.0 + grad_x * grad_x + grad_y * grad_y)


def shade_kernel(z_ref, beside_ref, out_ref):
    z = z_ref[...]
    out_ref[:ROWS, :] = shade_of(z, pltpu.roll(z, 1, 0), pltpu.roll(z, ROWS - 1, 0)).astype(BF16)
    row = iota((8, TILE), 0)
    border = jnp.where(row < 2, z[:8], jnp.where(row < 4, pltpu.roll(z[ROWS - 8 :], 4, 0), F32(0)))
    edge = jnp.where(lax.axis_index("bands") == 0, beside_ref[ROWS - 1 :], beside_ref[:1])
    border = jnp.where(row == 4, edge, border)
    high = border.astype(BF16).astype(F32)
    out_ref[ROWS:, :] = jnp.concatenate([high, border - high], axis=0).astype(BF16)


def resample_kernel(recv_ref, out_ref, across_ref, meta_ref):
    row, col = iota((16, GROUP), 0), iota((16, GROUP), 1)
    pick = ones_where(col == CHUNK * row + 2 * CAP).astype(BF16)
    for g in range(OWNERS // 8):
        meta_ref[g * 8 : (g + 1) * 8, :] = dot(pick, recv_ref[g * GROUP : (g + 1) * GROUP, :])[:8]
    row, col = iota((2 * 64, GROUP), 0), iota((2 * 64, GROUP), 1)
    slot = row & 63
    pick = ones_where(col == CHUNK * (slot >> 3) + 2 * (slot & 7) + (row >> 6)).astype(BF16)
    for g in range(OWNERS // 8):
        parts = dot(pick, recv_ref[g * GROUP : (g + 1) * GROUP, :])
        across_ref[g * 64 : (g + 1) * 64, :HALF] = parts[:64].astype(BF16)
        across_ref[g * 64 : (g + 1) * 64, HALF:] = parts[64:].astype(BF16)
    slots = OWNERS * CAP
    meta = meta_ref[...]
    rolled = [meta] + [pltpu.roll(meta, HALF - CAP * f, 1) for f in range(1, FIELDS)]
    spread = ones_where(iota((HALF, slots), 0) == (iota((HALF, slots), 1) & 7)).astype(BF16)
    wide = dot(jnp.concatenate(rolled, axis=0).astype(BF16), spread)
    own_lane = iota((OWNERS, slots), 0) == (iota((OWNERS, slots), 1) >> 3)
    fields = [
        jnp.sum(jnp.where(own_lane, wide[f * OWNERS : (f + 1) * OWNERS], F32(0)), axis=0, keepdims=True)
        for f in range(FIELDS)
    ]
    block, inner = fields[0].astype(I32), fields[1].astype(I32)
    diff = iota((16, slots), 0) - inner
    here, after = jnp.zeros((16, slots), F32), jnp.zeros((16, slots), F32)
    for tap in range(KA):
        here = jnp.where(diff == tap, fields[2 + tap], here)
        after = jnp.where(diff + 16 == tap, fields[2 + tap], after)
    block = jnp.broadcast_to(block, (16, slots))
    across = across_ref[...]
    for tile in range(TILES):
        weights = jnp.concatenate(
            [
                jnp.where(block == p, here, jnp.where(block == p - 1, after, F32(0))).astype(BF16)
                for p in range(16 * tile, 16 * tile + 16)
            ],
            axis=0,
        )
        out_ref[tile * TILE : (tile + 1) * TILE, :] = dot(weights, across)


def finish_kernel(
    resampled_ref,
    mine_ref,
    theirs_ref,
    list_ref,
    out_ref,
    part_ref,
    far_ref,
    near_ref,
    border_ref,
    reduced_ref,
    column_ref,
):
    tile_me = lax.axis_index("tile")
    band_me = lax.axis_index("bands")
    core_me, x_me = lax.rem(band_me, 2), lax.div(band_me, 2)

    def two_blocks(tile, rows):
        mine = mine_ref[tile ^ x_me, rows, :].astype(F32)
        theirs = theirs_ref[tile ^ x_me, rows, :].astype(F32)
        return jnp.where(core_me == 0, mine, theirs), jnp.where(core_me == 0, theirs, mine)

    for tile in range(TILES):
        for i, part in enumerate(two_blocks(tile, slice(ROWS, ROWS + 16))):
            exact = part[:8] + part[8:]
            for f in range(5):
                border_ref[f, 2 * tile + i : 2 * tile + i + 1, :] = exact[f : f + 1]
    first, second, before_last, last, edge = [border_ref[f] for f in range(5)]
    row = iota((8, TILE), 0)
    first_shade = shade_of(first, jnp.where(row == 0, edge[0:1], pltpu.roll(last, 1, 0)), second)
    last_shade = shade_of(last, before_last, jnp.where(row == 7, edge[7:8], pltpu.roll(first, 7, 0)))

    cols_of = ones_where((iota((TILE, HALF), 0) >> 1) == iota((TILE, HALF), 1)).astype(BF16)
    for tile in range(TILES):
        shade = []
        for i, block in enumerate(two_blocks(tile, slice(0, ROWS))):
            b = 2 * tile + i
            shade.append(jnp.where(row == 0, first_shade[b : b + 1], block[:8]))
            shade.append(block[8:-8])
            shade.append(jnp.where(row == 7, last_shade[b : b + 1], block[-8:]))
        rows = slice(tile * TILE, (tile + 1) * TILE)
        finished = (resampled_ref[rows, :] * jnp.concatenate(shade, axis=0)).astype(BF16)
        out_ref[rows, :] = finished
        column_ref[rows, :] = dot(finished, cols_of)
        even, odd = [column_ref[pl.ds(tile * TILE + i, HALF, stride=2), :] for i in range(2)]
        reduced_ref[tile] = (even + odd) * 0.25

    part_ref[...] = jnp.zeros(part_ref.shape, F32)
    near_ref[...] = jnp.zeros(near_ref.shape, BF16)
    far_ref[...] = jnp.zeros(far_ref.shape, BF16)
    side = 1 - 2 * lax.rem(tile_me, 2)
    counts = [jnp.int32(0), jnp.int32(0)]
    codes = [[jnp.int32(0), jnp.int32(0)], [jnp.int32(0), jnp.int32(0)]]
    for tile in range(TILES):
        offset = list_ref[tile, 0] - tile_me
        code = list_ref[tile, 1] * 4 + list_ref[tile, 2]

        @pl.when(offset == 0)
        def _(tile=tile, code=code):
            part_ref[code] = part_ref[code] + reduced_ref[tile]

        for way, (step, ref) in enumerate(((side, near_ref), (-side, far_ref))):
            goes = offset == step
            rank = jnp.minimum(counts[way], 1)

            @pl.when(goes)
            def _(tile=tile, rank=rank, ref=ref):
                ref[pl.ds(pl.multiple_of(rank * HALF, HALF), HALF), :] = reduced_ref[tile].astype(BF16)

            for s in range(2):
                codes[way][s] = jnp.where(goes & (rank == s), code + 1, codes[way][s])
            counts[way] = counts[way] + goes.astype(I32)
    eighth = iota((16, HALF), 0) < 8
    for way, ref in enumerate((near_ref, far_ref)):
        ref[2 * HALF :, :] = jnp.where(eighth, codes[way][0], codes[way][1]).astype(F32).astype(BF16)


def store_kernel(finished_ref, out_ref, sem):
    copy = pltpu.make_async_copy(finished_ref, out_ref, sem)
    copy.start()
    copy.wait()


def combine_kernel(part_ref, far_ref, near_ref, out_ref, stage_ref, sems):
    arrived = []
    for ref in (far_ref, near_ref):
        codes = ref[2 * HALF :, :].astype(F32)
        for s in range(2):
            arrived.append((codes[8 * s : 8 * s + 1], ref[s * HALF : (s + 1) * HALF, :].astype(F32)))
    copies = []
    for level in range(2):
        for quadrant in range(4):
            place = 4 * level + quadrant
            total = part_ref[place]
            for code, tile in arrived:
                total = total + jnp.where(code == F32(place + 1), tile, F32(0))
            top, left = quadrant // 2 * HALF, quadrant % 2 * HALF
            stage_ref[level, top : top + HALF, left : left + HALF] = total.astype(BF16)
        copy = pltpu.make_async_copy(stage_ref.at[level], out_ref.at[level], sems.at[level])
        copy.start()
        copies.append(copy)
    for copy in copies:
        copy.wait()


def call(kernel, outs, ins, scratch=(), cost=None, params=PARAMS, out_specs=None):
    return pl.pallas_call(
        kernel,
        out_shape=outs,
        in_specs=ins,
        out_specs=out_specs or jax.tree.map(lambda _: VMEM, outs),
        scratch_shapes=scratch,
        compiler_params=params,
        cost_estimate=cost,
    )


def swap(value, first):
    pairs = [(i, i + 1) for i in range(first, lax.axis_size("tile") - 1, 2)]
    return lax.ppermute(value, "tile", pairs + [(j, i) for i, j in pairs])


def exchange(value, mask):
    return lax.ppermute(value, "bands", [(i, i ^ mask) for i in range(lax.axis_size("bands"))])


def shards(scene_rows, row_dest, row_pos, along_taps, across_taps, elevation, pyramid_list):
    shape = jax.ShapeDtypeStruct
    outgoing = call(
        prep_kernel,
        shape((OWNERS * CHUNK, HALF), BF16),
        [VMEM] * 5,
        [pltpu.VMEM((OWNERS * CHUNK, HALF), BF16), pltpu.SemaphoreType.DMA((2,))],
        params=pltpu.CompilerParams(vmem_limit_bytes=60 * 1024 * 1024),
        out_specs=pl.BlockSpec(memory_space=pl.ANY),
    )(
        scene_rows[0],
        row_dest.T,
        row_pos.T,
        along_taps.transpose(1, 2, 0),
        across_taps[0].T,
    )
    both, bands = ("tile", "bands"), lax.axis_size("bands")
    pairs = [(bands * t - 1, bands * t) for t in range(1, lax.axis_size("tile"))]
    pairs = pairs + [(j, i) for i, j in pairs]
    beside = lax.ppermute(elevation, both, pairs)
    outgoing, elevation = lax.optimization_barrier((outgoing, elevation))
    units = outgoing.reshape(OWNERS * CHUNK // 2, 2, HALF)
    received = lax.all_to_all(units, "tile", split_axis=0, concat_axis=0, tiled=True)
    received = received.reshape(OWNERS * CHUNK, HALF)

    shade = call(shade_kernel, shape((ROWS + 16, TILE), BF16), [VMEM] * 2, cost=WINDOW)(elevation, beside)
    mine = jnp.stack([shade, exchange(shade, 2), exchange(shade, 4), exchange(shade, 6)])
    theirs = exchange(mine, 1)
    resampled = call(
        resample_kernel,
        shape((TILES * TILE, TILE), F32),
        [VMEM],
        [pltpu.VMEM((OWNERS * CAP, TILE), BF16), pltpu.VMEM((OWNERS, HALF), F32)],
        pl.CostEstimate(flops=400_000_000, bytes_accessed=1_500_000, transcendentals=0),
    )(received)
    finished, part, far, near = call(
        finish_kernel,
        (
            shape((TILES * TILE, TILE), BF16),
            shape((8, HALF, HALF), F32),
            shape((PAYLOAD, HALF), BF16),
            shape((PAYLOAD, HALF), BF16),
        ),
        [VMEM, VMEM, VMEM, SMEM],
        [
            pltpu.VMEM((5, 8, TILE), F32),
            pltpu.VMEM((TILES, HALF, HALF), F32),
            pltpu.VMEM((TILES * TILE, HALF), F32),
        ],
    )(resampled, mine, theirs, pyramid_list)
    far, near = swap(far, 1), swap(near, 0)
    finished = call(
        store_kernel,
        shape((TILES * TILE, TILE), BF16),
        [VMEM],
        [pltpu.SemaphoreType.DMA],
        pl.CostEstimate(flops=0, bytes_accessed=1_000_000, transcendentals=0),
        out_specs=pl.BlockSpec(memory_space=pl.ANY),
    )(finished)
    pyramid = call(
        combine_kernel,
        shape((2, TILE, TILE), BF16),
        [VMEM] * 3,
        [pltpu.VMEM((2, TILE, TILE), BF16), pltpu.SemaphoreType.DMA((2,))],
        out_specs=pl.BlockSpec(memory_space=pl.ANY),
    )(part, far, near)
    return (finished[None], pyramid[None])


def solution(mesh):
    in_specs = (
        P("bands", "tile", None),
        P("tile", None),
        P("tile", None),
        P("tile", None, None),
        P("bands", None, None),
        P(("tile", "bands"), None),
        P("tile", None),
    )
    out_specs = (P("bands", "tile", None), P("bands", "tile", None, None))
    return jax.shard_map(shards, mesh=mesh, in_specs=in_specs, out_specs=out_specs, check_vma=False)
```
